128 devices in a mesh: blk: 16 (over z, y_lo, core), win: 8 (over y_hi, x).
Axes of the slice: x: 4, y: 4 (y_hi: 2, y_lo: 2; y = y_hi * 2 + y_lo), z: 4, core: 2. Of those that a mesh axis runs over, the one named last changes fastest.
Arguments:
- spectra: bfloat16 [1920, 2, 64, 2048], P('win', None, None, 'blk'), may hold values from -0.76171875 to 0.76171875
- partners: int32 [3, 16], replicated, may hold values from 0 to 15, as said below
Outputs:
- cross: float32 [3, 16, 128, 2, 64, 128], P(None, 'blk', 'win')
The draws below stay inside these ranges and needn't reach their ends.
Inputs may be any that keep to these rules, and one draw needn't show every extreme that they name: Each row of partners pairs the blocks: partners[r, partners[r, b]] = b and partners[r, b] != b; no two blocks are paired in two different rounds.
All inputs are finite; a program needn't handle non-finite values.
Results may differ from the reference program's by a relative error of at most 0.0003.
Values may be sent and summed in bfloat16 or wider, within the bound.
A program may use at most 192 MiB of HBM per device.

```python
import jax
import jax.numpy as jnp
from jax import lax

F = 64
CB = 128
WIN_DEV = 240
ROUNDS = 3
BLOCKS = 16
CHANNELS = 2048
WINDOWS = 1920
N_WIN = 8


def draw_partners(key, part):
    key = jax.random.fold_in(key, 11)
    first, second = jax.random.split(key)
    count = BLOCKS
    odd = count - 1
    labels = jax.random.permutation(first, count).astype(jnp.int32)
    chosen = jax.random.permutation(second, odd)[:ROUNDS].astype(jnp.int32)
    places = jnp.arange(count, dtype=jnp.int32)
    facing = (2 * chosen[:, None] - places[None, :]) % odd
    mate = jnp.where(facing == places[None, :], odd, facing)
    mate = jnp.where(places[None, :] == odd, chosen[:, None], mate).astype(jnp.int32)
    result = jnp.zeros((ROUNDS, count), jnp.int32).at[:, labels].set(labels[mate])
    return result


def levels(rng, shape, pieces, smallest, high):
    def one(axis_at, blocks):
        draws = jax.random.uniform(jax.random.fold_in(jax.random.fold_in(rng, 6), axis_at), (blocks,), jnp.float32, smallest / len(pieces), high / len(pieces))
        return jnp.repeat(jnp.exp(draws), shape[axis_at] // blocks).reshape((-1,) + (1,) * (len(shape) - axis_at - 1))

    gain = one(*pieces[0])
    for cut in pieces[1:]:
        gain = gain * one(*cut)
    return gain


def scatter_about(rng, extent, width, limit, cuts=(), kind=jnp.bfloat16):
    gain = levels(rng, extent, cuts, -0.22, 0.18) if cuts else 1.0
    entries = jax.random.normal(rng, extent, jnp.float32) * width * gain
    return jnp.minimum(jnp.maximum(entries, -limit), limit).astype(kind)


def setup_inputs(seed: int = 0) -> dict:
    key_list = jax.random.split(jax.random.key(seed), 3)
    spectra = scatter_about(key_list[0], (WINDOWS, 2, F, CHANNELS), ((2 * WINDOWS) ** -0.25), 0.76171875, ((0, 8), (3, 16)))
    partners = draw_partners(jax.random.fold_in(key_list[2], 71), 0)
    return dict(spectra=spectra, partners=partners)


def block_cross(spectra, own_start, mate_start):
    mine = lax.dynamic_slice_in_dim(spectra, own_start, CB, 3).astype(jnp.float32)
    other = lax.dynamic_slice_in_dim(spectra, mate_start, CB, 3).astype(jnp.float32)
    mine = mine.reshape(N_WIN, WIN_DEV, 2, F, CB)
    other = other.reshape(N_WIN, WIN_DEV, 2, F, CB)
    real = jnp.einsum("gwfa,gwfc->gafc", mine[:, :, 0], other[:, :, 0]) + jnp.einsum("gwfa,gwfc->gafc", mine[:, :, 1], other[:, :, 1])
    imag = jnp.einsum("gwfa,gwfc->gafc", mine[:, :, 0], other[:, :, 1]) - jnp.einsum("gwfa,gwfc->gafc", mine[:, :, 1], other[:, :, 0])
    parts = jnp.stack([real, imag], 2)
    return jnp.sum(parts, 0)


def reference(spectra, partners):
    blocks = jnp.arange(BLOCKS, dtype=jnp.int32)
    rounds_out = []
    for step in range(ROUNDS):
        def one_block(pair):
            block, mate = pair
            return block_cross(spectra, (block * CB).astype(jnp.int32), (mate * CB).astype(jnp.int32))
        rounds_out.append(lax.map(one_block, (blocks, partners[step].astype(jnp.int32))))
    return jnp.stack(rounds_out, 0)
```

```python
import jax
import jax.numpy as jnp
from jax import lax
from jax.experimental import pallas as pl
from jax.experimental.pallas import tpu as pltpu
from jax.sharding import Mesh, PartitionSpec as P


def cross_kernel(mates, x_ref, p_ref, o_ref):
    def wide(ref):
        v = ref[0]
        rows = v.shape[0] * v.shape[2]
        return jnp.concatenate(
            [v[:, 0].reshape(rows, v.shape[3]), v[:, 1].reshape(rows, v.shape[3])], axis=1
        )

    left, right = wide(x_ref), wide(p_ref)
    g = lax.dot_general(
        left, right, (((0,), (0,)), ((), ())), preferred_element_type=jnp.float32
    )
    n = x_ref.shape[-1]
    real = g[:n, :n] + g[n:, n:]
    imag = g[:n, n:] - g[n:, :n]
    o_ref[0, :, 0, :, 0, :] = real.reshape(o_ref.shape[1], o_ref.shape[3], n)
    o_ref[0, :, 0, :, 1, :] = imag.reshape(o_ref.shape[1], o_ref.shape[3], n)


def cross(own, every, mates, groups):
    blocks, win, _, w, n = own.shape
    rounds = mates.shape[0]
    return pl.pallas_call(
        cross_kernel,
        grid_spec=pltpu.PrefetchScalarGridSpec(
            num_scalar_prefetch=1,
            grid=(blocks, rounds),
            in_specs=[
                pl.BlockSpec((1, win, 2, w, n), lambda b, r, m: (b, 0, 0, 0, 0)),
                pl.BlockSpec((1, win, 2, w, n), lambda b, r, m: (m[r, b], 0, 0, 0, 0)),
            ],
            out_specs=pl.BlockSpec(
                (1, groups, 1, n // groups, 2, n), lambda b, r, m: (b, 0, r, 0, 0, 0)
            ),
        ),
        out_shape=jax.ShapeDtypeStruct((blocks, groups, rounds, n // groups, 2, n), jnp.float32),
        compiler_params=pltpu.CompilerParams(vmem_limit_bytes=40 << 20),
        cost_estimate=pl.CostEstimate(
            flops=blocks * rounds * win * w * n * n * 8,
            bytes_accessed=blocks * (rounds + 1) * win * w * n * 4,
            transcendentals=0,
        ),
    )(mates, own, every)


def shards(spectra, partners):
    w, _, f, n = spectra.shape
    core = lax.axis_index("core")
    x = jnp.transpose(spectra, (2, 1, 0, 3))
    got = lax.all_to_all(x, ("zy", "win"), 0, 0, tiled=True)
    zy, win = 8, 8
    own = got.reshape(zy, win, 2, w, n)
    every = lax.all_gather(own, "core", axis=1, tiled=False).reshape(2 * zy, win, 2, w, n)
    mates = lax.dynamic_index_in_dim(
        partners.reshape(partners.shape[0], zy, 2), core, 2, keepdims=False
    )
    part = cross(own, every, mates, win)
    part = part.reshape((zy * win,) + part.shape[2:])
    back = lax.all_to_all(part, ("zy", "win"), 0, 0, tiled=True)
    return jnp.transpose(back, (1, 2, 3, 0, 4))[:, None]


def solution(mesh):
    split = Mesh(mesh.devices.reshape(8, 2, 8), ("zy", "core", "win"))
    return jax.shard_map(
        shards,
        mesh=split,
        in_specs=(P("win", None, None, ("zy", "core")), P()),
        out_specs=P(None, ("zy", "core"), "win", None, None, None),
        check_vma=False,
    )
```

```python
import functools

import jax
import jax.numpy as jnp
from jax import lax
from jax.experimental import pallas as pl
from jax.experimental.pallas import tpu as pltpu
from jax.sharding import PartitionSpec as P

MESH = pl.DeviceIdType.MESH
SIDE = 4
STEPS = (1, 3, 2)
ALL = slice(None)


def position():
    blk, win = lax.axis_index("blk"), lax.axis_index("win")
    return (win % 4, win // 4 * 2 + blk // 2 % 2, blk // 4), blk % 2


def device(place, core):
    x, y, z = place
    return (z * 4 + y % 2 * 2 + core, y // 2 * 4 + x)


def neighbour(place, core, axis, step):
    moved = list(place)
    moved[axis] = (moved[axis] + step) % SIDE
    return device(moved, core)


def pick(**chosen):
    return tuple(chosen.get(name, ALL) for name in "xyz")


class Exchange:
    def __init__(self, place, core, source, first, second, target, sems):
        self.place, self.core = place, core
        self.source, self.first, self.second, self.target = source, first, second, target
        self.sems = sems
        self.one, self.two, self.three, self.kept, self.sent = {}, {}, {}, {}, []

    def send(self, src, dst, which, at, axis, step):
        send_sem, recv_sem = self.sems[2 * which], self.sems[2 * which + 1]
        copy = pltpu.make_async_remote_copy(
            src_ref=src,
            dst_ref=dst,
            send_sem=send_sem.at[at],
            recv_sem=recv_sem.at[at],
            device_id=neighbour(self.place, self.core, axis, step),
            device_id_type=MESH,
        )
        copy.start()
        self.sent.append(copy)
        return copy

    def keep(self, src, dst, which, at):
        copy = pltpu.make_async_copy(src, dst, self.sems[2 * which + 1].at[at])
        copy.start()
        return copy

    def axes(self, t):
        return t, (t + 1) % 3, (t + 2) % 3

    def phase_one(self, t, d1):
        a1, _, _ = self.axes(t)
        there = (self.place[a1] + d1) % SIDE
        self.one[t, d1] = self.send(
            self.source(t, pick(**{"xyz"[a1]: there})),
            self.first.at[t, self.place[a1]],
            0,
            (t, d1),
            a1,
            d1,
        )

    def phase_two(self, t, d1):
        a1, a2, _ = self.axes(t)
        origin = (self.place[a1] - d1) % SIDE
        for d2 in STEPS + (0,):
            there = (self.place[a2] + d2) % SIDE
            if d1 == 0:
                src = self.source(t, pick(**{"xyz"[a1]: origin, "xyz"[a2]: there}))
            else:
                rest = [there if axis == a2 else ALL for axis in range(3) if axis != a1]
                src = self.first.at[(t, origin, *rest)]
            dst = self.second.at[t, self.place[a2], origin]
            at = (t, d1, d2)
            if d2 == 0:
                self.two[at] = self.keep(src, dst, 1, at)
            else:
                self.two[at] = self.send(src, dst, 1, at, a2, d2)

    def phase_three(self, t, d2):
        a1, a2, a3 = self.axes(t)
        origin = (self.place[a2] - d2) % SIDE
        for d1 in (0,) + STEPS:
            self.arrive(self.two[t, d1, d2], d2)
        for d3 in STEPS + (0,):
            there = (self.place[a3] + d3) % SIDE
            src = self.second.at[t, origin, :, there]
            dst = self.target(t, pick(**{"xyz"[a2]: origin, "xyz"[a3]: self.place[a3]}))
            at = (t, d2, d3)
            if d3 == 0:
                self.three[at] = self.keep(src, dst, 2, at)
            else:
                self.three[at] = self.send(src, dst, 2, at, a3, d3)

    def landed(self, t, d2, d3):
        _, a2, a3 = self.axes(t)
        return pick(
            **{
                "xyz"[a2]: (self.place[a2] - d2) % SIDE,
                "xyz"[a3]: (self.place[a3] - d3) % SIDE,
            }
        )

    def arrive(self, copy, step):
        if step == 0:
            copy.wait()
        else:
            copy.wait_recv()

    def finish(self):
        for copy in self.sent:
            copy.wait_send()


def kernel(
    mates, x_ref, o_ref, first, second, every, turned, part, first_out, second_out, *sems
):
    place, core = position()
    sibling = device(place, 1 - core)
    rounds = 3
    w = every.shape[-2]
    n = every.shape[-1]
    shift = x_ref.shape[-2] // 3

    barrier = pltpu.get_barrier_semaphore()
    for axis in range(3):
        for step in STEPS:
            pl.semaphore_signal(
                barrier,
                inc=1,
                device_id=neighbour(place, core, axis, step),
                device_id_type=MESH,
            )
    pl.semaphore_signal(barrier, inc=1, device_id=sibling, device_id_type=MESH)
    pl.semaphore_wait(barrier, 10)

    into = Exchange(
        place,
        core,
        lambda t, at: x_ref.at[(*at, ALL, pl.ds(t * shift, shift))],
        first,
        second,
        lambda t, at: every.at[(core, t, *at)],
        sems[0:6],
    )
    for d1 in STEPS:
        for t in range(3):
            into.phase_one(t, d1)
    for t in range(3):
        into.phase_two(t, 0)
    for d1 in STEPS:
        for t in range(3):
            into.arrive(into.one[t, d1], d1)
            into.phase_two(t, d1)
    for d2 in (0,) + STEPS:
        for t in range(3):
            into.phase_three(t, d2)
    swaps = []
    for d2 in (0,) + STEPS:
        for d3 in (0,) + STEPS:
            for t in range(3):
                into.arrive(into.three[t, d2, d3], d3)
                here = every.at[(core, t, *into.landed(t, d2, d3))]
                copy = pltpu.make_async_remote_copy(
                    src_ref=here,
                    dst_ref=here,
                    send_sem=sems[12].at[t, d2, d3],
                    recv_sem=sems[13].at[t, d2, d3],
                    device_id=sibling,
                    device_id_type=MESH,
                )
                copy.start()
                swaps.append(copy)
    for copy in swaps:
        copy.wait_recv()

    def wide(owner, y_lo, z):
        halves = []
        for q in range(2):
            rows = []
            for t in range(3):
                for y_hi in range(2):
                    for x in range(SIDE):
                        rows.append(every[owner, t, x, 2 * y_hi + y_lo, z, q])
            halves.append(jnp.concatenate(rows, axis=0))
        return jnp.concatenate(halves, axis=1)

    back = Exchange(
        place,
        core,
        lambda t, at: part.at[(t, *at)],
        first_out,
        second_out,
        lambda t, at: o_ref.at[(t, *at)],
        sems[6:12],
    )
    for r in range(rounds):

        @pl.loop(0, 2 * SIDE)
        def block(i):
            z, y_lo = i // 2, i % 2
            if r == 0:
                turned[i] = wide(core, y_lo, z).T
            mate = mates[r, i * 2 + core]
            g = jnp.dot(
                turned[i],
                wide(mate % 2, mate // 2 % 2, mate // 4),
                preferred_element_type=jnp.float32,
            )
            real = g[:n, :n] + g[n:, n:]
            imag = g[:n, n:] - g[n:, :n]
            rows = part.shape[-2]
            for y_hi in range(2):
                for x in range(SIDE):
                    cut = slice((y_hi * SIDE + x) * rows, (y_hi * SIDE + x + 1) * rows)
                    part[r, x, 2 * y_hi + y_lo, z, 0] = real[cut]
                    part[r, x, 2 * y_hi + y_lo, z, 1] = imag[cut]

        for d1 in STEPS:
            back.phase_one(r, d1)
        back.phase_two(r, 0)
    for d1 in STEPS:
        for t in range(3):
            back.arrive(back.one[t, d1], d1)
            back.phase_two(t, d1)
    for d2 in (0,) + STEPS:
        for t in range(3):
            back.phase_three(t, d2)
    for d2 in (0,) + STEPS:
        for d3 in (0,) + STEPS:
            for t in range(3):
                back.arrive(back.three[t, d2, d3], d3)
    into.finish()
    back.finish()
    for copy in swaps:
        copy.wait_send()


def cross(x, partners):
    _, _, _, _, windows, n = x.shape
    rows = n // 8
    third = windows // 3
    grid = (SIDE, SIDE)
    sems = pltpu.SemaphoreType.DMA
    exchange_sems = [sems((3, 4)), sems((3, 4))] + [sems((3, 4, 4))] * 4
    return pl.pallas_call(
        kernel,
        out_shape=jax.ShapeDtypeStruct((3, SIDE, SIDE, SIDE, 2, rows, n), jnp.float32),
        in_specs=[
            pl.BlockSpec(memory_space=pltpu.SMEM),
            pl.BlockSpec(memory_space=pl.ANY),
        ],
        out_specs=pl.BlockSpec(memory_space=pl.ANY),
        scratch_shapes=[
            pltpu.VMEM((3, SIDE, *grid, 2, third, n), jnp.bfloat16),
            pltpu.VMEM((3, SIDE, *grid, 2, third, n), jnp.bfloat16),
            pltpu.VMEM((2, 3, SIDE, *grid, 2, third, n), jnp.bfloat16),
            pltpu.VMEM((8, 2 * n, 8 * windows), jnp.bfloat16),
            pltpu.VMEM((3, SIDE, *grid, 2, rows, n), jnp.float32),
            pltpu.VMEM((3, SIDE, *grid, 2, rows, n), jnp.float32),
            pltpu.VMEM((3, SIDE, *grid, 2, rows, n), jnp.float32),
        ]
        + exchange_sems * 2
        + [sems((3, 4, 4))] * 2,
        compiler_params=pltpu.CompilerParams(
            collective_id=0, has_side_effects=True, vmem_limit_bytes=60 << 20
        ),
        cost_estimate=pl.CostEstimate(
            flops=24 * 8 * windows * n * n * 8,
            bytes_accessed=16 << 20,
            transcendentals=0,
        ),
        name="cross",
    )(partners, x)


def shards(spectra, partners):
    w, _, f, n = spectra.shape
    x = jnp.transpose(spectra, (2, 1, 0, 3)).reshape(SIDE, SIDE, SIDE, 2, w, n)
    back = cross(x, partners)
    back = back.reshape(3, f, 2, n // 8, n)
    return jnp.transpose(back, (0, 3, 2, 1, 4))[:, None]


def solution(mesh):
    return jax.shard_map(
        shards,
        mesh=mesh,
        in_specs=(P("win", None, None, "blk"), P()),
        out_specs=P(None, "blk", "win", None, None, None),
        check_vma=False,
    )
```

```python
import functools

import jax
import jax.numpy as jnp
from jax import lax
from jax.experimental import pallas as pl
from jax.experimental.pallas import tpu as pltpu
from jax.sharding import PartitionSpec as P

MESH = pl.DeviceIdType.MESH
SIDE = 4
STEPS = (1, 3, 2)
ALL = slice(None)


def position():
    blk, win = lax.axis_index("blk"), lax.axis_index("win")
    return (win % 4, win // 4 * 2 + blk // 2 % 2, blk // 4), blk % 2


def device(place, core):
    x, y, z = place
    return (z * 4 + y % 2 * 2 + core, y // 2 * 4 + x)


def neighbour(place, core, axis, step):
    moved = list(place)
    moved[axis] = (moved[axis] + step) % SIDE
    return device(moved, core)


def pick(**chosen):
    return tuple(chosen.get(name, ALL) for name in "xyz")


class Exchange:
    def __init__(self, place, core, source, first, second, target, sems):
        self.place, self.core = place, core
        self.source, self.first, self.second, self.target = source, first, second, target
        self.sems = sems
        self.one, self.two, self.three, self.kept, self.sent = {}, {}, {}, {}, []

    def send(self, src, dst, which, at, axis, step):
        send_sem, recv_sem = self.sems[2 * which], self.sems[2 * which + 1]
        copy = pltpu.make_async_remote_copy(
            src_ref=src,
            dst_ref=dst,
            send_sem=send_sem.at[at],
            recv_sem=recv_sem.at[at],
            device_id=neighbour(self.place, self.core, axis, step),
            device_id_type=MESH,
        )
        copy.start()
        self.sent.append(copy)
        return copy

    def keep(self, src, dst, which, at):
        copy = pltpu.make_async_copy(src, dst, self.sems[2 * which + 1].at[at])
        copy.start()
        return copy

    def axes(self, t):
        return t, (t + 1) % 3, (t + 2) % 3

    def phase_one(self, t, d1):
        a1, _, _ = self.axes(t)
        there = (self.place[a1] + d1) % SIDE
        self.one[t, d1] = self.send(
            self.source(t, pick(**{"xyz"[a1]: there})),
            self.first.at[t, self.place[a1]],
            0,
            (t, d1),
            a1,
            d1,
        )

    def phase_two(self, t, d1):
        a1, a2, _ = self.axes(t)
        origin = (self.place[a1] - d1) % SIDE
        for d2 in STEPS + (0,):
            there = (self.place[a2] + d2) % SIDE
            if d1 == 0:
                src = self.source(t, pick(**{"xyz"[a1]: origin, "xyz"[a2]: there}))
            else:
                rest = [there if axis == a2 else ALL for axis in range(3) if axis != a1]
                src = self.first.at[(t, origin, *rest)]
            dst = self.second.at[t, self.place[a2], origin]
            at = (t, d1, d2)
            if d2 == 0:
                self.two[at] = self.keep(src, dst, 1, at)
            else:
                self.two[at] = self.send(src, dst, 1, at, a2, d2)

    def phase_three(self, t, d2):
        a1, a2, a3 = self.axes(t)
        origin = (self.place[a2] - d2) % SIDE
        for d1 in (0,) + STEPS:
            self.arrive(self.two[t, d1, d2], d2)
        for d3 in STEPS + (0,):
            there = (self.place[a3] + d3) % SIDE
            src = self.second.at[t, origin, :, there]
            dst = self.target(t, pick(**{"xyz"[a2]: origin, "xyz"[a3]: self.place[a3]}))
            at = (t, d2, d3)
            if d3 == 0:
                self.three[at] = self.keep(src, dst, 2, at)
            else:
                self.three[at] = self.send(src, dst, 2, at, a3, d3)

    def landed(self, t, d2, d3):
        _, a2, a3 = self.axes(t)
        return pick(
            **{
                "xyz"[a2]: (self.place[a2] - d2) % SIDE,
                "xyz"[a3]: (self.place[a3] - d3) % SIDE,
            }
        )

    def arrive(self, copy, step):
        if step == 0:
            copy.wait()
        else:
            copy.wait_recv()

    def finish(self):
        for copy in self.sent:
            copy.wait_send()


def kernel(
    mates,
    spectra,
    o_ref,
    stage,
    x_ref,
    first,
    second,
    every,
    turned,
    part,
    first_out,
    second_out,
    stage_sem,
    *sems,
):
    place, core = position()
    sibling = device(place, 1 - core)
    rounds = 3
    w = every.shape[-2]
    n = every.shape[-1]
    shift = x_ref.shape[-2] // 3
    slots, cut_rows = stage.shape[:2]
    pieces = x_ref.shape[-2] // cut_rows

    def load(i):
        return pltpu.make_async_copy(
            spectra.at[pl.ds(i * cut_rows, cut_rows)],
            stage.at[i % slots],
            stage_sem.at[i % slots],
        )

    for i in range(slots):
        load(i).start()

    barrier = pltpu.get_barrier_semaphore()
    for axis in range(3):
        for step in STEPS:
            pl.semaphore_signal(
                barrier,
                inc=1,
                device_id=neighbour(place, core, axis, step),
                device_id_type=MESH,
            )
    pl.semaphore_signal(barrier, inc=1, device_id=sibling, device_id_type=MESH)

    def relayout(t):
        @pl.loop(t * pieces // 3, (t + 1) * pieces // 3)
        def piece(i):
            load(i).wait()
            rows = pl.ds(pl.multiple_of(i * cut_rows, cut_rows), cut_rows)
            for q in range(2):
                for x in range(SIDE):
                    v = stage[i % slots, :, q, x * 16 : (x + 1) * 16, :]
                    v = jnp.swapaxes(v, 0, 1).reshape(SIDE, SIDE, cut_rows, n)
                    x_ref[x, :, :, q, rows, :] = v

            @pl.when(i + slots < pieces)
            def _():
                load(i + slots).start()

    relayout(0)
    relayout(1)
    pl.semaphore_wait(barrier, 10)

    into = Exchange(
        place,
        core,
        lambda t, at: x_ref.at[(*at, ALL, pl.ds(t * shift, shift))],
        first,
        second,
        lambda t, at: every.at[(core, t, *at)],
        sems[0:6],
    )
    for d1 in STEPS:
        for t in range(2):
            into.phase_one(t, d1)
    relayout(2)
    for d1 in STEPS:
        into.phase_one(2, d1)
    for t in range(3):
        into.phase_two(t, 0)
    for d1 in STEPS:
        for t in range(3):
            into.arrive(into.one[t, d1], d1)
            into.phase_two(t, d1)
    for d2 in (0,) + STEPS:
        for t in range(3):
            into.phase_three(t, d2)
    swaps = []
    for d2 in (0,) + STEPS:
        for d3 in (0,) + STEPS:
            for t in range(3):
                into.arrive(into.three[t, d2, d3], d3)
                here = every.at[(core, t, *into.landed(t, d2, d3))]
                copy = pltpu.make_async_remote_copy(
                    src_ref=here,
                    dst_ref=here,
                    send_sem=sems[12].at[t, d2, d3],
                    recv_sem=sems[13].at[t, d2, d3],
                    device_id=sibling,
                    device_id_type=MESH,
                )
                copy.start()
                swaps.append(copy)
    for copy in swaps:
        copy.wait_recv()

    def wide(owner, y_lo, z):
        halves = []
        for q in range(2):
            rows = []
            for t in range(3):
                for y_hi in range(2):
                    for x in range(SIDE):
                        rows.append(every[owner, t, x, 2 * y_hi + y_lo, z, q])
            halves.append(jnp.concatenate(rows, axis=0))
        return jnp.concatenate(halves, axis=1)

    back = Exchange(
        place,
        core,
        lambda t, at: part.at[(t, *at)],
        first_out,
        second_out,
        lambda t, at: o_ref.at[(t, *at)],
        sems[6:12],
    )
    for r in range(rounds):

        @pl.loop(0, 2 * SIDE)
        def block(i):
            z, y_lo = i // 2, i % 2
            if r == 0:
                turned[i] = wide(core, y_lo, z).T
            mate = mates[r, i * 2 + core]
            g = jnp.dot(
                turned[i],
                wide(mate % 2, mate // 2 % 2, mate // 4),
                preferred_element_type=jnp.float32,
            )
            real = g[:n, :n] + g[n:, n:]
            imag = g[:n, n:] - g[n:, :n]
            rows = part.shape[-2]
            for y_hi in range(2):
                for x in range(SIDE):
                    cut = slice((y_hi * SIDE + x) * rows, (y_hi * SIDE + x + 1) * rows)
                    part[r, x, 2 * y_hi + y_lo, z, 0] = real[cut]
                    part[r, x, 2 * y_hi + y_lo, z, 1] = imag[cut]

        for d1 in STEPS:
            back.phase_one(r, d1)
        back.phase_two(r, 0)
    for d1 in STEPS:
        for t in range(3):
            back.arrive(back.one[t, d1], d1)
            back.phase_two(t, d1)
    for d2 in (0,) + STEPS:
        for t in range(3):
            back.phase_three(t, d2)
    for d2 in (0,) + STEPS:
        for d3 in (0,) + STEPS:
            for t in range(3):
                back.arrive(back.three[t, d2, d3], d3)
    into.finish()
    back.finish()
    for copy in swaps:
        copy.wait_send()


def cross(x, partners):
    windows, _, _, n = x.shape
    rows = n // 8
    third = windows // 3
    grid = (SIDE, SIDE)
    sems = pltpu.SemaphoreType.DMA
    exchange_sems = [sems((3, 4)), sems((3, 4))] + [sems((3, 4, 4))] * 4
    return pl.pallas_call(
        kernel,
        out_shape=jax.ShapeDtypeStruct((3, SIDE, SIDE, SIDE, 2, rows, n), jnp.float32),
        in_specs=[
            pl.BlockSpec(memory_space=pltpu.SMEM),
            pl.BlockSpec(memory_space=pl.ANY),
        ],
        out_specs=pl.BlockSpec(memory_space=pl.ANY),
        scratch_shapes=[
            pltpu.VMEM((4, 16, 2, SIDE**3, n), jnp.bfloat16),
            pltpu.VMEM((SIDE, *grid, 2, windows, n), jnp.bfloat16),
            pltpu.VMEM((3, SIDE, *grid, 2, third, n), jnp.bfloat16),
            pltpu.VMEM((3, SIDE, *grid, 2, third, n), jnp.bfloat16),
            pltpu.VMEM((2, 3, SIDE, *grid, 2, third, n), jnp.bfloat16),
            pltpu.VMEM((8, 2 * n, 8 * windows), jnp.bfloat16),
            pltpu.VMEM((3, SIDE, *grid, 2, rows, n), jnp.float32),
            pltpu.VMEM((3, SIDE, *grid, 2, rows, n), jnp.float32),
            pltpu.VMEM((3, SIDE, *grid, 2, rows, n), jnp.float32),
        ]
        + [sems((4,))]
        + exchange_sems * 2
        + [sems((3, 4, 4))] * 2,
        compiler_params=pltpu.CompilerParams(
            collective_id=0, has_side_effects=True, vmem_limit_bytes=60 << 20
        ),
        cost_estimate=pl.CostEstimate(
            flops=24 * 8 * windows * n * n * 8,
            bytes_accessed=16 << 20,
            transcendentals=0,
        ),
        name="cross",
    )(partners, x)


def shards(spectra, partners):
    w, _, f, n = spectra.shape
    back = cross(spectra, partners)
    back = back.reshape(3, f, 2, n // 8, n)
    return jnp.transpose(back, (0, 3, 2, 1, 4))[:, None]


def solution(mesh):
    return jax.shard_map(
        shards,
        mesh=mesh,
        in_specs=(P("win", None, None, "blk"), P()),
        out_specs=P(None, "blk", "win", None, None, None),
        check_vma=False,
    )
```

```python
import functools

import jax
import jax.numpy as jnp
from jax import lax
from jax.experimental import pallas as pl
from jax.experimental.pallas import tpu as pltpu
from jax.sharding import PartitionSpec as P

MESH = pl.DeviceIdType.MESH
SIDE = 4
STEPS = (1, 3, 2)
ALL = slice(None)
CODES = 32767.0
TINY = 1e-36


def position():
    blk, win = lax.axis_index("blk"), lax.axis_index("win")
    return (win % 4, win // 4 * 2 + blk // 2 % 2, blk // 4), blk % 2


def device(place, core):
    x, y, z = place
    return (z * 4 + y % 2 * 2 + core, y // 2 * 4 + x)


def neighbour(place, core, axis, step):
    moved = list(place)
    moved[axis] = (moved[axis] + step) % SIDE
    return device(moved, core)


def pick(**chosen):
    return tuple(chosen.get(name, ALL) for name in "xyz")


def encode(value, scale):
    root = jnp.sqrt(jnp.sqrt(jnp.abs(value) * scale))
    code = (root * CODES + 0.5).astype(jnp.int32)
    return jnp.where(value < 0, -code, code).astype(jnp.int16)


class Exchange:
    def __init__(self, place, core, source, first, second, target, sems):
        self.place, self.core = place, core
        self.source, self.first, self.second, self.target = source, first, second, target
        self.sems = sems
        self.one, self.two, self.three, self.kept, self.sent = {}, {}, {}, {}, []

    def send(self, src, dst, which, at, axis, step):
        send_sem, recv_sem = self.sems[2 * which], self.sems[2 * which + 1]
        copy = pltpu.make_async_remote_copy(
            src_ref=src,
            dst_ref=dst,
            send_sem=send_sem.at[at],
            recv_sem=recv_sem.at[at],
            device_id=neighbour(self.place, self.core, axis, step),
            device_id_type=MESH,
        )
        copy.start()
        self.sent.append(copy)
        return copy

    def keep(self, src, dst, which, at):
        copy = pltpu.make_async_copy(src, dst, self.sems[2 * which + 1].at[at])
        copy.start()
        return copy

    def axes(self, t):
        return t, (t + 1) % 3, (t + 2) % 3

    def phase_one(self, t, d1):
        a1, _, _ = self.axes(t)
        there = (self.place[a1] + d1) % SIDE
        self.one[t, d1] = self.send(
            self.source(t, pick(**{"xyz"[a1]: there})),
            self.first.at[t, self.place[a1]],
            0,
            (t, d1),
            a1,
            d1,
        )

    def phase_two(self, t, d1):
        a1, a2, _ = self.axes(t)
        origin = (self.place[a1] - d1) % SIDE
        for d2 in STEPS + (0,):
            there = (self.place[a2] + d2) % SIDE
            if d1 == 0:
                src = self.source(t, pick(**{"xyz"[a1]: origin, "xyz"[a2]: there}))
            else:
                rest = [there if axis == a2 else ALL for axis in range(3) if axis != a1]
                src = self.first.at[(t, origin, *rest)]
            dst = self.second.at[t, self.place[a2], origin]
            at = (t, d1, d2)
            if d2 == 0:
                self.two[at] = self.keep(src, dst, 1, at)
            else:
                self.two[at] = self.send(src, dst, 1, at, a2, d2)

    def phase_three(self, t, d2):
        a1, a2, a3 = self.axes(t)
        origin = (self.place[a2] - d2) % SIDE
        for d1 in (0,) + STEPS:
            self.arrive(self.two[t, d1, d2], d2)
        for d3 in STEPS + (0,):
            there = (self.place[a3] + d3) % SIDE
            src = self.second.at[t, origin, :, there]
            dst = self.target(t, pick(**{"xyz"[a2]: origin, "xyz"[a3]: self.place[a3]}))
            at = (t, d2, d3)
            if d3 == 0:
                self.three[at] = self.keep(src, dst, 2, at)
            else:
                self.three[at] = self.send(src, dst, 2, at, a3, d3)

    def landed(self, t, d2, d3):
        _, a2, a3 = self.axes(t)
        return pick(
            **{
                "xyz"[a2]: (self.place[a2] - d2) % SIDE,
                "xyz"[a3]: (self.place[a3] - d3) % SIDE,
            }
        )

    def arrive(self, copy, step):
        if step == 0:
            copy.wait()
        else:
            copy.wait_recv()

    def finish(self):
        for copy in self.sent:
            copy.wait_send()


def kernel(
    mates,
    spectra,
    o_ref,
    scales,
    stage,
    x_ref,
    first,
    second,
    every,
    turned,
    product,
    largest,
    part,
    first_out,
    second_out,
    stage_sem,
    scale_keep,
    scale_send,
    scale_recv,
    *sems,
):
    place, core = position()
    sibling = device(place, 1 - core)
    rounds = 3
    w = every.shape[-2]
    n = every.shape[-1]
    shift = x_ref.shape[-2] // 3
    slots, cut_rows = stage.shape[:2]
    pieces = x_ref.shape[-2] // cut_rows

    def load(i):
        return pltpu.make_async_copy(
            spectra.at[pl.ds(i * cut_rows, cut_rows)],
            stage.at[i % slots],
            stage_sem.at[i % slots],
        )

    for i in range(slots):
        load(i).start()

    barrier = pltpu.get_barrier_semaphore()
    for axis in range(3):
        for step in STEPS:
            pl.semaphore_signal(
                barrier,
                inc=1,
                device_id=neighbour(place, core, axis, step),
                device_id_type=MESH,
            )
    pl.semaphore_signal(barrier, inc=1, device_id=sibling, device_id_type=MESH)

    def relayout(t):
        @pl.loop(t * pieces // 3, (t + 1) * pieces // 3)
        def piece(i):
            load(i).wait()
            rows = pl.ds(pl.multiple_of(i * cut_rows, cut_rows), cut_rows)
            for q in range(2):
                for x in range(SIDE):
                    v = stage[i % slots, :, q, x * 16 : (x + 1) * 16, :]
                    v = jnp.swapaxes(v, 0, 1).reshape(SIDE, SIDE, cut_rows, n)
                    x_ref[x, :, :, q, rows, :] = v

            @pl.when(i + slots < pieces)
            def _():
                load(i + slots).start()

    relayout(0)
    relayout(1)
    pl.semaphore_wait(barrier, 10)

    into = Exchange(
        place,
        core,
        lambda t, at: x_ref.at[(*at, ALL, pl.ds(t * shift, shift))],
        first,
        second,
        lambda t, at: every.at[(core, t, *at)],
        sems[0:6],
    )
    for d1 in STEPS:
        for t in range(2):
            into.phase_one(t, d1)
    relayout(2)
    for d1 in STEPS:
        into.phase_one(2, d1)
    for t in range(3):
        into.phase_two(t, 0)
    for d1 in STEPS:
        for t in range(3):
            into.arrive(into.one[t, d1], d1)
            into.phase_two(t, d1)
    for d2 in (0,) + STEPS:
        for t in range(3):
            into.phase_three(t, d2)
    swaps = []
    for d2 in (0,) + STEPS:
        for d3 in (0,) + STEPS:
            for t in range(3):
                into.arrive(into.three[t, d2, d3], d3)
                here = every.at[(core, t, *into.landed(t, d2, d3))]
                copy = pltpu.make_async_remote_copy(
                    src_ref=here,
                    dst_ref=here,
                    send_sem=sems[12].at[t, d2, d3],
                    recv_sem=sems[13].at[t, d2, d3],
                    device_id=sibling,
                    device_id_type=MESH,
                )
                copy.start()
                swaps.append(copy)
    for copy in swaps:
        copy.wait_recv()

    def wide(owner, y_lo, z):
        halves = []
        for q in range(2):
            rows = []
            for t in range(3):
                for y_hi in range(2):
                    for x in range(SIDE):
                        rows.append(every[owner, t, x, 2 * y_hi + y_lo, z, q])
            halves.append(jnp.concatenate(rows, axis=0))
        return jnp.concatenate(halves, axis=1)

    back = Exchange(
        place,
        core,
        lambda t, at: part.at[(t, *at)],
        first_out,
        second_out,
        lambda t, at: o_ref.at[(t, *at)],
        sems[6:12],
    )
    for r in range(rounds):
        largest[r] = jnp.zeros_like(largest[r])

        @pl.loop(0, 2 * SIDE)
        def block(i):
            z, y_lo = i // 2, i % 2
            if r == 0:
                turned[i] = wide(core, y_lo, z).T
            mate = mates[r, i * 2 + core]
            g = jnp.dot(
                turned[i],
                wide(mate % 2, mate // 2 % 2, mate // 4),
                preferred_element_type=jnp.float32,
            )
            real = g[:n, :n] + g[n:, n:]
            imag = g[:n, n:] - g[n:, :n]
            both = jnp.maximum(jnp.abs(real), jnp.abs(imag)).reshape(-1, 8, n)
            largest[r] = jnp.maximum(largest[r], jnp.max(both, axis=0))
            rows = part.shape[-2]
            for y_hi in range(2):
                for x in range(SIDE):
                    cut = slice((y_hi * SIDE + x) * rows, (y_hi * SIDE + x + 1) * rows)
                    product[x, 2 * y_hi + y_lo, z, 0] = real[cut]
                    product[x, 2 * y_hi + y_lo, z, 1] = imag[cut]

        top = jnp.maximum(jnp.max(largest[r], keepdims=True), TINY)
        largest[r] = jnp.broadcast_to(top, largest.shape[1:])
        scale = 1.0 / jnp.broadcast_to(top, (1, n))

        @pl.loop(0, SIDE * SIDE)
        def code(i):
            for z in range(SIDE):
                for q in range(2):
                    part[r, i // SIDE, i % SIDE, z, q] = encode(
                        product[i // SIDE, i % SIDE, z, q], scale
                    )

        for d1 in STEPS:
            back.phase_one(r, d1)
        back.phase_two(r, 0)

    def scale_send_along(axis):
        at = tuple(ALL if other < axis else place[other] for other in range(3))
        here = scales.at[(ALL, *at)]
        copies = []
        for step in STEPS:
            copy = pltpu.make_async_remote_copy(
                src_ref=here,
                dst_ref=here,
                send_sem=scale_send.at[axis, step],
                recv_sem=scale_recv.at[axis, step],
                device_id=neighbour(place, core, axis, step),
                device_id_type=MESH,
            )
            copy.start()
            copies.append(copy)
        return copies

    kept = pltpu.make_async_copy(
        largest.at[:, pl.ds(0, 1)], scales.at[(ALL, *place)], scale_keep
    )
    kept.start()
    kept.wait()
    shared = scale_send_along(0)
    for d1 in STEPS:
        for t in range(3):
            back.arrive(back.one[t, d1], d1)
            back.phase_two(t, d1)
    for copy in shared[:3]:
        copy.wait_recv()
    shared += scale_send_along(1)
    for d2 in (0,) + STEPS:
        for t in range(3):
            back.phase_three(t, d2)
    for copy in shared[3:6]:
        copy.wait_recv()
    shared += scale_send_along(2)
    for d2 in (0,) + STEPS:
        for d3 in (0,) + STEPS:
            for t in range(3):
                back.arrive(back.three[t, d2, d3], d3)
    for copy in shared[6:]:
        copy.wait_recv()
    for copy in shared:
        copy.wait_send()
    into.finish()
    back.finish()
    for copy in swaps:
        copy.wait_send()


def decode_kernel(codes, scales, o_ref):
    n = codes.shape[-1]
    share = codes[0, :, 0].astype(jnp.int32).astype(jnp.float32) * (1.0 / CODES)
    value = share * share * (share * jnp.abs(share))
    value = jnp.swapaxes(value, 0, 1)
    o_ref[0, 0, :, 0] = value * scales[0].reshape(1, -1, n)


def decode(codes, scales):
    rounds, f, _, rows, n = codes.shape
    return pl.pallas_call(
        decode_kernel,
        grid=(rounds, 2),
        out_shape=jax.ShapeDtypeStruct((rounds, 1, rows, 2, f, n), jnp.float32),
        in_specs=[
            pl.BlockSpec((1, f, 1, rows, n), lambda r, q: (r, 0, q, 0, 0)),
            pl.BlockSpec((1, f, 1, n), lambda r, q: (r, 0, 0, 0)),
        ],
        out_specs=pl.BlockSpec((1, 1, rows, 1, f, n), lambda r, q: (r, 0, 0, q, 0, 0)),
        compiler_params=pltpu.CompilerParams(vmem_limit_bytes=16 << 20),
        name="decode",
    )(codes, scales)


def cross(x, partners):
    windows, _, _, n = x.shape
    rows = n // 8
    third = windows // 3
    grid = (SIDE, SIDE)
    sems = pltpu.SemaphoreType.DMA
    exchange_sems = [sems((3, 4)), sems((3, 4))] + [sems((3, 4, 4))] * 4
    return pl.pallas_call(
        kernel,
        out_shape=[
            jax.ShapeDtypeStruct((3, SIDE, *grid, 2, rows, n), jnp.int16),
            jax.ShapeDtypeStruct((3, SIDE, *grid, 1, n), jnp.float32),
        ],
        in_specs=[
            pl.BlockSpec(memory_space=pltpu.SMEM),
            pl.BlockSpec(memory_space=pl.ANY),
        ],
        out_specs=[pl.BlockSpec(memory_space=pl.ANY)] * 2,
        scratch_shapes=[
            pltpu.VMEM((4, 16, 2, SIDE**3, n), jnp.bfloat16),
            pltpu.VMEM((SIDE, *grid, 2, windows, n), jnp.bfloat16),
            pltpu.VMEM((3, SIDE, *grid, 2, third, n), jnp.bfloat16),
            pltpu.VMEM((3, SIDE, *grid, 2, third, n), jnp.bfloat16),
            pltpu.VMEM((2, 3, SIDE, *grid, 2, third, n), jnp.bfloat16),
            pltpu.VMEM((8, 2 * n, 8 * windows), jnp.bfloat16),
            pltpu.VMEM((SIDE, *grid, 2, rows, n), jnp.float32),
            pltpu.VMEM((3, 8, n), jnp.float32),
            pltpu.VMEM((3, SIDE, *grid, 2, rows, n), jnp.int16),
            pltpu.VMEM((3, SIDE, *grid, 2, rows, n), jnp.int16),
            pltpu.VMEM((3, SIDE, *grid, 2, rows, n), jnp.int16),
        ]
        + [sems((4,)), sems, sems((3, 4)), sems((3, 4))]
        + exchange_sems * 2
        + [sems((3, 4, 4))] * 2,
        compiler_params=pltpu.CompilerParams(
            collective_id=0, has_side_effects=True, vmem_limit_bytes=60 << 20
        ),
        cost_estimate=pl.CostEstimate(
            flops=24 * 8 * windows * n * n * 8,
            bytes_accessed=16 << 20,
            transcendentals=0,
        ),
        name="cross",
    )(partners, x)


def shards(spectra, partners):
    w, _, f, n = spectra.shape
    codes, scales = cross(spectra, partners)
    return decode(codes.reshape(3, f, 2, n // 8, n), scales.reshape(3, f, 1, n))


def solution(mesh):
    return jax.shard_map(
        shards,
        mesh=mesh,
        in_specs=(P("win", None, None, "blk"), P()),
        out_specs=P(None, "blk", "win", None, None, None),
        check_vma=False,
    )
```

```python
import functools

import jax
import jax.numpy as jnp
from jax import lax
from jax.experimental import pallas as pl
from jax.experimental.pallas import tpu as pltpu
from jax.sharding import PartitionSpec as P

MESH = pl.DeviceIdType.MESH
SIDE = 4
STEPS = (1, 3, 2)
ALL = slice(None)
SHARES = (48, 32)
CODES = 32767.0
TINY = 1e-36


def position():
    blk, win = lax.axis_index("blk"), lax.axis_index("win")
    return (win % 4, win // 4 * 2 + blk // 2 % 2, blk // 4), blk % 2


def device(place, core):
    x, y, z = place
    return (z * 4 + y % 2 * 2 + core, y // 2 * 4 + x)


def neighbour(place, core, axis, step):
    moved = list(place)
    moved[axis] = (moved[axis] + step) % SIDE
    return device(moved, core)


def pick(**chosen):
    return tuple(chosen.get(name, ALL) for name in "xyz")


def encode(value, scale):
    share = jnp.abs(value) * scale + 1e-20
    root = share * lax.rsqrt(share)
    root = root * lax.rsqrt(root)
    code = (root * CODES + 0.5).astype(jnp.int32)
    return jnp.where(value < 0, -code, code).astype(jnp.int16)


class Exchange:
    def __init__(self, place, core, source, first, second, target, sems):
        self.place, self.core = place, core
        self.source, self.first, self.second, self.target = source, first, second, target
        self.sems = sems
        self.one, self.two, self.three, self.kept, self.sent = {}, {}, {}, {}, []

    def send(self, src, dst, which, at, axis, step):
        send_sem, recv_sem = self.sems[2 * which], self.sems[2 * which + 1]
        copy = pltpu.make_async_remote_copy(
            src_ref=src,
            dst_ref=dst,
            send_sem=send_sem.at[at],
            recv_sem=recv_sem.at[at],
            device_id=neighbour(self.place, self.core, axis, step),
            device_id_type=MESH,
        )
        copy.start()
        self.sent.append(copy)
        return copy

    def keep(self, src, dst, which, at):
        copy = pltpu.make_async_copy(src, dst, self.sems[2 * which + 1].at[at])
        copy.start()
        return copy

    def axes(self, t):
        return t, (t + 1) % 3, (t + 2) % 3

    def phase_one(self, t, d1):
        a1, _, _ = self.axes(t)
        there = (self.place[a1] + d1) % SIDE
        self.one[t, d1] = self.send(
            self.source(t, pick(**{"xyz"[a1]: there})),
            self.first.at[t, self.place[a1]],
            0,
            (t, d1),
            a1,
            d1,
        )

    def phase_two(self, t, d1):
        a1, a2, _ = self.axes(t)
        origin = (self.place[a1] - d1) % SIDE
        for d2 in STEPS + (0,):
            there = (self.place[a2] + d2) % SIDE
            if d1 == 0:
                src = self.source(t, pick(**{"xyz"[a1]: origin, "xyz"[a2]: there}))
            else:
                rest = [there if axis == a2 else ALL for axis in range(3) if axis != a1]
                src = self.first.at[(t, origin, *rest)]
            dst = self.second.at[t, self.place[a2], origin]
            at = (t, d1, d2)
            if d2 == 0:
                self.two[at] = self.keep(src, dst, 1, at)
            else:
                self.two[at] = self.send(src, dst, 1, at, a2, d2)

    def phase_three(self, t, d2):
        a1, a2, a3 = self.axes(t)
        origin = (self.place[a2] - d2) % SIDE
        for d1 in (0,) + STEPS:
            self.arrive(self.two[t, d1, d2], d2)
        for d3 in STEPS + (0,):
            there = (self.place[a3] + d3) % SIDE
            src = self.second.at[t, origin, :, there]
            dst = self.target(t, pick(**{"xyz"[a2]: origin, "xyz"[a3]: self.place[a3]}))
            at = (t, d2, d3)
            if d3 == 0:
                self.three[at] = self.keep(src, dst, 2, at)
            else:
                self.three[at] = self.send(src, dst, 2, at, a3, d3)

    def landed(self, t, d2, d3):
        _, a2, a3 = self.axes(t)
        return pick(
            **{
                "xyz"[a2]: (self.place[a2] - d2) % SIDE,
                "xyz"[a3]: (self.place[a3] - d3) % SIDE,
            }
        )

    def arrive(self, copy, step):
        if step == 0:
            copy.wait()
        else:
            copy.wait_recv()

    def finish(self):
        for copy in self.sent:
            copy.wait_send()


def kernel(mates, spectra, o_ref, scales, *scratch):
    scratch = list(scratch)

    def take(count):
        taken = scratch[:count]
        del scratch[:count]
        return taken

    (stage,) = take(1)
    shares = len(SHARES)
    ready, first, second, every = take(shares), take(shares), take(shares), take(shares)
    turned, product, largest, part, first_out, second_out = take(6)
    stage_sem, scale_keep, scale_send, scale_recv = take(4)
    swap_send, swap_recv = take(shares), take(shares)
    place, core = position()
    sibling = device(place, 1 - core)
    rounds, n = product.shape[0], product.shape[-1]
    slots, cut_rows = stage.shape[:2]
    third = sum(SHARES)
    order = [
        (h, t, t * third + sum(SHARES[:h]) + k * cut_rows, k * cut_rows)
        for h in range(shares)
        for t in range(3)
        for k in range(SHARES[h] // cut_rows)
    ]

    def load(j):
        return pltpu.make_async_copy(
            spectra.at[pl.ds(order[j][2], cut_rows)],
            stage.at[j % slots],
            stage_sem.at[j % slots],
        )

    for j in range(slots):
        load(j).start()

    barrier = pltpu.get_barrier_semaphore()
    for axis in range(3):
        for step in STEPS:
            pl.semaphore_signal(
                barrier,
                inc=1,
                device_id=neighbour(place, core, axis, step),
                device_id_type=MESH,
            )
    pl.semaphore_signal(barrier, inc=1, device_id=sibling, device_id_type=MESH)

    def relayout(share, thirds):
        for j, (h, t, _, row) in enumerate(order):
            if h != share or t not in thirds:
                continue
            load(j).wait()

            @pl.loop(0, 2 * SIDE)
            def turn(i):
                q, x = i // SIDE, i % SIDE
                v = stage[j % slots, :, q, pl.ds(pl.multiple_of(x * 16, 16), 16), :]
                v = jnp.swapaxes(v, 0, 1).reshape(SIDE, SIDE, cut_rows, n)
                ready[h][t, x, :, :, q, row : row + cut_rows, :] = v

            if j + slots < len(order):
                load(j + slots).start()

    into = [
        Exchange(
            place,
            core,
            lambda t, at, h=h: ready[h].at[(t, *at)],
            first[h],
            second[h],
            lambda t, at, h=h: every[h].at[(core, t, *at)],
            take(6),
        )
        for h in range(shares)
    ]
    back = Exchange(
        place,
        core,
        lambda t, at: part.at[(t, *at)],
        first_out,
        second_out,
        lambda t, at: o_ref.at[(t, *at)],
        take(6),
    )
    swaps = []

    def swap(h, d2):
        for d3 in (0,) + STEPS:
            for t in range(3):
                into[h].arrive(into[h].three[t, d2, d3], d3)
                here = every[h].at[(core, t, *into[h].landed(t, d2, d3))]
                copy = pltpu.make_async_remote_copy(
                    src_ref=here,
                    dst_ref=here,
                    send_sem=swap_send[h].at[t, d2, d3],
                    recv_sem=swap_recv[h].at[t, d2, d3],
                    device_id=sibling,
                    device_id_type=MESH,
                )
                copy.start()
                swaps.append((h, copy))

    def swapped(h):
        for share, copy in swaps:
            if share == h:
                copy.wait_recv()

    def wide(h, owner, y_lo, z):
        halves = []
        for q in range(2):
            rows = []
            for t in range(3):
                for y_hi in range(2):
                    for x in range(SIDE):
                        rows.append(every[h][owner, t, x, 2 * y_hi + y_lo, z, q])
            halves.append(jnp.concatenate(rows, axis=0))
        return jnp.concatenate(halves, axis=1)

    def multiply(h, r, i):
        depth = 24 * SHARES[h]
        z, y_lo = i // 2, i % 2
        if r == 0:
            turned[i, :, :depth] = wide(h, core, y_lo, z).T
        mate = mates[r, i * 2 + core]
        g = jnp.dot(
            turned[i, :, :depth],
            wide(h, mate % 2, mate // 2 % 2, mate // 4),
            preferred_element_type=jnp.float32,
        )
        sums = (g[:n, :n] + g[n:, n:], g[:n, n:] - g[n:, :n])
        rows = product.shape[-2]
        at = lambda k: (r, k % SIDE, k // SIDE * 2 + y_lo, z)
        if h:
            old = [
                jnp.concatenate([product[(*at(k), q)] for k in range(2 * SIDE)], axis=0)
                for q in range(2)
            ]
            sums = (sums[0] + old[0], sums[1] + old[1])
        for k in range(2 * SIDE):
            for q in range(2):
                product[(*at(k), q)] = sums[q][k * rows : (k + 1) * rows]
        return jnp.maximum(jnp.abs(sums[0]), jnp.abs(sums[1])).reshape(-1, 8, n)

    def products(h, r):
        @pl.loop(0, 2)
        def blocks(j):
            for k in range(SIDE):
                multiply(h, r, j * SIDE + k)

    def code(r, i, scale):
        for z in range(SIDE):
            for q in range(2):
                part[r, i // SIDE, i % SIDE, z, q] = encode(
                    product[r, i // SIDE, i % SIDE, z, q], scale
                )

    def scale_of(r, top):
        top = jnp.maximum(jnp.max(jnp.max(top, axis=0), keepdims=True), TINY)
        largest[r] = jnp.broadcast_to(top, largest.shape[1:])
        return 1.0 / jnp.broadcast_to(top, (1, n))

    for h in range(shares):
        for thirds in ((0, 1), (2,)) if h == 0 else ((0, 1, 2),):
            relayout(h, thirds)
            if h == 0 and thirds[0] == 0:
                pl.semaphore_wait(barrier, 10)
            for d1 in STEPS:
                for t in thirds:
                    into[h].phase_one(t, d1)
        for t in range(3):
            into[h].phase_two(t, 0)
    for h in range(shares):
        for d1 in STEPS:
            for t in range(3):
                into[h].arrive(into[h].one[t, d1], d1)
                into[h].phase_two(t, d1)
    for h in range(shares):
        if h >= 2:
            for d2 in (0,) + STEPS:
                swap(h - 2, d2)
            swapped(h - 2)
            for r in range(rounds):
                products(h - 2, r)
        for d2 in (0,) + STEPS:
            for t in range(3):
                into[h].phase_three(t, d2)
    last = shares - 1
    for d2 in (0,) + STEPS:
        swap(last - 1, d2)
    swapped(last - 1)
    products(last - 1, 0)
    swap(last, 0)
    products(last - 1, 1)
    swap(last, STEPS[0])
    products(last - 1, 2)
    swap(last, STEPS[1])
    swap(last, STEPS[2])
    swapped(shares - 1)

    scale = None
    for r in range(rounds + 1):
        tops = []
        for i in range(2 * SIDE):
            if r < rounds:
                tops.append(jnp.max(multiply(last, r, i), axis=0))
            if r:
                code(r - 1, 2 * i, scale)
                code(r - 1, 2 * i + 1, scale)
        if r < rounds:
            scale = scale_of(r, jnp.stack(tops))
        if r:
            for d1 in STEPS:
                back.phase_one(r - 1, d1)
            back.phase_two(r - 1, 0)

    def scale_send_along(axis):
        at = tuple(ALL if other < axis else place[other] for other in range(3))
        here = scales.at[(ALL, *at)]
        copies = []
        for step in STEPS:
            copy = pltpu.make_async_remote_copy(
                src_ref=here,
                dst_ref=here,
                send_sem=scale_send.at[axis, step],
                recv_sem=scale_recv.at[axis, step],
                device_id=neighbour(place, core, axis, step),
                device_id_type=MESH,
            )
            copy.start()
            copies.append(copy)
        return copies

    kept = pltpu.make_async_copy(
        largest.at[:, pl.ds(0, 1)], scales.at[(ALL, *place)], scale_keep
    )
    kept.start()
    kept.wait()
    shared = scale_send_along(0)
    for d1 in STEPS:
        for t in range(3):
            back.arrive(back.one[t, d1], d1)
            back.phase_two(t, d1)
    for copy in shared[:3]:
        copy.wait_recv()
    shared += scale_send_along(1)
    for d2 in (0,) + STEPS:
        for t in range(3):
            back.phase_three(t, d2)
    for copy in shared[3:6]:
        copy.wait_recv()
    shared += scale_send_along(2)
    for d2 in (0,) + STEPS:
        for d3 in (0,) + STEPS:
            for t in range(3):
                back.arrive(back.three[t, d2, d3], d3)
    for copy in shared[6:]:
        copy.wait_recv()
    for copy in shared:
        copy.wait_send()
    for exchange in into:
        exchange.finish()
    back.finish()
    for _, copy in swaps:
        copy.wait_send()


def decode_kernel(codes, scales, o_ref):
    n = codes.shape[-1]
    share = codes[0, :, 0].astype(jnp.int32).astype(jnp.float32) * (1.0 / CODES)
    value = share * share * (share * jnp.abs(share))
    value = jnp.swapaxes(value, 0, 1)
    o_ref[0, 0, :, 0] = value * scales[0].reshape(1, -1, n)


def decode(codes, scales):
    rounds, f, _, rows, n = codes.shape
    return pl.pallas_call(
        decode_kernel,
        grid=(rounds, 2),
        out_shape=jax.ShapeDtypeStruct((rounds, 1, rows, 2, f, n), jnp.float32),
        in_specs=[
            pl.BlockSpec((1, f, 1, rows, n), lambda r, q: (r, 0, q, 0, 0)),
            pl.BlockSpec((1, f, 1, n), lambda r, q: (r, 0, 0, 0)),
        ],
        out_specs=pl.BlockSpec((1, 1, rows, 1, f, n), lambda r, q: (r, 0, 0, q, 0, 0)),
        compiler_params=pltpu.CompilerParams(vmem_limit_bytes=60 << 20),
        name="decode",
    )(codes, scales)


def cross(x, partners):
    windows, _, _, n = x.shape
    rows = n // 8
    grid = (SIDE, SIDE)
    sems = pltpu.SemaphoreType.DMA
    exchange_sems = [sems((3, 4)), sems((3, 4))] + [sems((3, 4, 4))] * 4
    return pl.pallas_call(
        kernel,
        out_shape=[
            jax.ShapeDtypeStruct((3, SIDE, *grid, 2, rows, n), jnp.int16),
            jax.ShapeDtypeStruct((3, SIDE, *grid, 1, n), jnp.float32),
        ],
        in_specs=[
            pl.BlockSpec(memory_space=pltpu.SMEM),
            pl.BlockSpec(memory_space=pl.ANY),
        ],
        out_specs=[pl.BlockSpec(memory_space=pl.ANY)] * 2,
        scratch_shapes=[pltpu.VMEM((4, 16, 2, SIDE**3, n), jnp.bfloat16)]
        + [pltpu.VMEM((3, SIDE, *grid, 2, share, n), jnp.bfloat16) for share in SHARES] * 3
        + [pltpu.VMEM((2, 3, SIDE, *grid, 2, share, n), jnp.bfloat16) for share in SHARES]
        + [
            pltpu.VMEM((8, 2 * n, 24 * max(SHARES)), jnp.bfloat16),
            pltpu.VMEM((3, SIDE, *grid, 2, rows, n), jnp.float32),
            pltpu.VMEM((3, 8, n), jnp.float32),
        ]
        + [pltpu.VMEM((3, SIDE, *grid, 2, rows, n), jnp.int16)] * 3
        + [sems((4,)), sems, sems((3, 4)), sems((3, 4))]
        + [sems((3, 4, 4))] * (2 * len(SHARES))
        + exchange_sems * (len(SHARES) + 1),
        compiler_params=pltpu.CompilerParams(
            collective_id=0, has_side_effects=True, vmem_limit_bytes=60 << 20
        ),
        cost_estimate=pl.CostEstimate(
            flops=24 * 8 * windows * n * n * 8,
            bytes_accessed=16 << 20,
            transcendentals=0,
        ),
        name="cross",
    )(partners, x)


def shards(spectra, partners):
    w, _, f, n = spectra.shape
    codes, scales = cross(spectra, partners)
    return decode(codes.reshape(3, f, 2, n // 8, n), scales.reshape(3, f, 1, n))


def solution(mesh):
    return jax.shard_map(
        shards,
        mesh=mesh,
        in_specs=(P("win", None, None, "blk"), P()),
        out_specs=P(None, "blk", "win", None, None, None),
        check_vma=False,
    )
```

```python
import functools

import jax
import jax.numpy as jnp
from jax import lax
from jax.experimental import pallas as pl
from jax.experimental.pallas import tpu as pltpu
from jax.sharding import PartitionSpec as P

MESH = pl.DeviceIdType.MESH
SIDE = 4
STEPS = (1, 3, 2)
ALL = slice(None)
SHARES = (48, 32)
CODES = 32767.0
TINY = 1e-36


def position():
    blk, win = lax.axis_index("blk"), lax.axis_index("win")
    return (win % 4, win // 4 * 2 + blk // 2 % 2, blk // 4), blk % 2


def device(place, core):
    x, y, z = place
    return (z * 4 + y % 2 * 2 + core, y // 2 * 4 + x)


def neighbour(place, core, axis, step):
    moved = list(place)
    moved[axis] = (moved[axis] + step) % SIDE
    return device(moved, core)


def pick(**chosen):
    return tuple(chosen.get(name, ALL) for name in "xyz")


def encode(value, scale):
    share = jnp.abs(value) * scale + 1e-20
    root = share * lax.rsqrt(share)
    root = root * lax.rsqrt(root)
    code = (root * CODES + 0.5).astype(jnp.int32)
    return jnp.where(value < 0, -code, code).astype(jnp.int16)


class Exchange:
    def __init__(self, place, core, source, first, second, target, sems):
        self.place, self.core = place, core
        self.source, self.first, self.second, self.target = source, first, second, target
        self.sems = sems
        self.one, self.two, self.three, self.kept, self.sent = {}, {}, {}, {}, []

    def send(self, src, dst, which, at, axis, step):
        send_sem, recv_sem = self.sems[2 * which], self.sems[2 * which + 1]
        copy = pltpu.make_async_remote_copy(
            src_ref=src,
            dst_ref=dst,
            send_sem=send_sem.at[at],
            recv_sem=recv_sem.at[at],
            device_id=neighbour(self.place, self.core, axis, step),
            device_id_type=MESH,
        )
        copy.start()
        self.sent.append(copy)
        return copy

    def keep(self, src, dst, which, at):
        copy = pltpu.make_async_copy(src, dst, self.sems[2 * which + 1].at[at])
        copy.start()
        return copy

    def axes(self, t):
        return t, (t + 1) % 3, (t + 2) % 3

    def phase_one(self, t, d1):
        a1, _, _ = self.axes(t)
        there = (self.place[a1] + d1) % SIDE
        self.one[t, d1] = self.send(
            self.source(t, pick(**{"xyz"[a1]: there})),
            self.first.at[t, self.place[a1]],
            0,
            (t, d1),
            a1,
            d1,
        )

    def phase_two(self, t, d1):
        a1, a2, _ = self.axes(t)
        origin = (self.place[a1] - d1) % SIDE
        for d2 in STEPS + (0,):
            there = (self.place[a2] + d2) % SIDE
            if d1 == 0:
                src = self.source(t, pick(**{"xyz"[a1]: origin, "xyz"[a2]: there}))
            else:
                rest = [there if axis == a2 else ALL for axis in range(3) if axis != a1]
                src = self.first.at[(t, origin, *rest)]
            dst = self.second.at[t, self.place[a2], origin]
            at = (t, d1, d2)
            if d2 == 0:
                self.two[at] = self.keep(src, dst, 1, at)
            else:
                self.two[at] = self.send(src, dst, 1, at, a2, d2)

    def phase_three(self, t, d2):
        a1, a2, a3 = self.axes(t)
        origin = (self.place[a2] - d2) % SIDE
        for d1 in (0,) + STEPS:
            self.arrive(self.two[t, d1, d2], d2)
        for d3 in STEPS + (0,):
            there = (self.place[a3] + d3) % SIDE
            src = self.second.at[t, origin, :, there]
            dst = self.target(t, pick(**{"xyz"[a2]: origin, "xyz"[a3]: self.place[a3]}))
            at = (t, d2, d3)
            if d3 == 0:
                self.three[at] = self.keep(src, dst, 2, at)
            else:
                self.three[at] = self.send(src, dst, 2, at, a3, d3)

    def landed(self, t, d2, d3):
        _, a2, a3 = self.axes(t)
        return pick(
            **{
                "xyz"[a2]: (self.place[a2] - d2) % SIDE,
                "xyz"[a3]: (self.place[a3] - d3) % SIDE,
            }
        )

    def arrive(self, copy, step):
        if step == 0:
            copy.wait()
        else:
            copy.wait_recv()

    def finish(self):
        for copy in self.sent:
            copy.wait_send()


def kernel(mates, spectra, o_ref, scales, *scratch):
    scratch = list(scratch)

    def take(count):
        taken = scratch[:count]
        del scratch[:count]
        return taken

    (stage,) = take(1)
    shares = len(SHARES)
    ready, first, second, every = take(shares), take(shares), take(shares), take(shares)
    turned, product, largest, part, first_out, second_out = take(6)
    stage_sem, scale_keep, scale_send, scale_recv = take(4)
    swap_send, swap_recv = take(shares), take(shares)
    place, core = position()
    sibling = device(place, 1 - core)
    rounds, n = product.shape[0], product.shape[-1]
    slots, cut_rows = stage.shape[:2]
    third = sum(SHARES)
    order = [
        (h, t, t * third + sum(SHARES[:h]) + k * cut_rows, k * cut_rows)
        for h in range(shares)
        for t in range(3)
        for k in range(SHARES[h] // cut_rows)
    ]

    def load(j):
        return pltpu.make_async_copy(
            spectra.at[pl.ds(order[j][2], cut_rows)],
            stage.at[j % slots],
            stage_sem.at[j % slots],
        )

    for j in range(slots):
        load(j).start()

    barrier = pltpu.get_barrier_semaphore()
    for axis in range(3):
        for step in STEPS:
            pl.semaphore_signal(
                barrier,
                inc=1,
                device_id=neighbour(place, core, axis, step),
                device_id_type=MESH,
            )
    pl.semaphore_signal(barrier, inc=1, device_id=sibling, device_id_type=MESH)

    def relayout(share, thirds):
        for j, (h, t, _, row) in enumerate(order):
            if h != share or t not in thirds:
                continue
            load(j).wait()

            @pl.loop(0, 2)
            def turn(q):
                for x in range(SIDE):
                    v = stage[j % slots, :, q, x * 16 : (x + 1) * 16, :]
                    v = jnp.swapaxes(v, 0, 1).reshape(SIDE, SIDE, cut_rows, n)
                    ready[h][t, x, :, :, q, row : row + cut_rows, :] = v

            if j + slots < len(order):
                load(j + slots).start()

    into = [
        Exchange(
            place,
            core,
            lambda t, at, h=h: ready[h].at[(t, *at)],
            first[h],
            second[h],
            lambda t, at, h=h: every[h].at[(core, t, *at)],
            take(6),
        )
        for h in range(shares)
    ]
    back = Exchange(
        place,
        core,
        lambda t, at: part.at[(t, *at)],
        first_out,
        second_out,
        lambda t, at: o_ref.at[(t, *at)],
        take(6),
    )
    swaps = []

    def swap(h, d2):
        for d3 in (0,) + STEPS:
            for t in range(3):
                into[h].arrive(into[h].three[t, d2, d3], d3)
                here = every[h].at[(core, t, *into[h].landed(t, d2, d3))]
                copy = pltpu.make_async_remote_copy(
                    src_ref=here,
                    dst_ref=here,
                    send_sem=swap_send[h].at[t, d2, d3],
                    recv_sem=swap_recv[h].at[t, d2, d3],
                    device_id=sibling,
                    device_id_type=MESH,
                )
                copy.start()
                swaps.append((h, copy))

    def swapped(h):
        for share, copy in swaps:
            if share == h:
                copy.wait_recv()

    def wide(h, owner, y_lo, z):
        halves = []
        for q in range(2):
            rows = []
            for t in range(3):
                for y_hi in range(2):
                    for x in range(SIDE):
                        rows.append(every[h][owner, t, x, 2 * y_hi + y_lo, z, q])
            halves.append(jnp.concatenate(rows, axis=0))
        return jnp.concatenate(halves, axis=1)

    def multiply(h, r, i):
        depth = 24 * SHARES[h]
        z, y_lo = i // 2, i % 2
        if r == 0:
            turned[i, :, :depth] = wide(h, core, y_lo, z).T
        mate = mates[r, i * 2 + core]
        g = jnp.dot(
            turned[i, :, :depth],
            wide(h, mate % 2, mate // 2 % 2, mate // 4),
            preferred_element_type=jnp.float32,
        )
        sums = (g[:n, :n] + g[n:, n:], g[:n, n:] - g[n:, :n])
        rows = product.shape[-2]
        at = lambda k: (r, k % SIDE, k // SIDE * 2 + y_lo, z)
        if h:
            old = [
                jnp.concatenate([product[(*at(k), q)] for k in range(2 * SIDE)], axis=0)
                for q in range(2)
            ]
            sums = (sums[0] + old[0], sums[1] + old[1])
        for k in range(2 * SIDE):
            for q in range(2):
                product[(*at(k), q)] = sums[q][k * rows : (k + 1) * rows]
        return jnp.maximum(jnp.abs(sums[0]), jnp.abs(sums[1])).reshape(-1, 8, n)

    def products(h, r):
        @pl.loop(0, 2)
        def blocks(j):
            for k in range(SIDE):
                multiply(h, r, j * SIDE + k)

    def code(r, i, scale):
        for z in range(SIDE):
            for q in range(2):
                part[r, i // SIDE, i % SIDE, z, q] = encode(
                    product[r, i // SIDE, i % SIDE, z, q], scale
                )

    def scale_of(r, top):
        top = jnp.maximum(jnp.max(jnp.max(top, axis=0), keepdims=True), TINY)
        largest[r] = jnp.broadcast_to(top, largest.shape[1:])
        return 1.0 / jnp.broadcast_to(top, (1, n))

    for h in range(shares):
        for thirds in ((0,), (1,), (2,)) if h == 0 else ((0, 1, 2),):
            relayout(h, thirds)
            if h == 0 and thirds[0] == 0:
                pl.semaphore_wait(barrier, 10)
            for d1 in STEPS:
                for t in thirds:
                    into[h].phase_one(t, d1)
        for t in range(3):
            into[h].phase_two(t, 0)
    for h in range(shares):
        for d1 in STEPS:
            for t in range(3):
                into[h].arrive(into[h].one[t, d1], d1)
                into[h].phase_two(t, d1)
    for h in range(shares):
        if h >= 2:
            for d2 in (0,) + STEPS:
                swap(h - 2, d2)
            swapped(h - 2)
            for r in range(rounds):
                products(h - 2, r)
        for d2 in (0,) + STEPS:
            for t in range(3):
                into[h].phase_three(t, d2)
    last = shares - 1
    for d2 in (0,) + STEPS:
        swap(last - 1, d2)
    swapped(last - 1)
    products(last - 1, 0)
    swap(last, 0)
    products(last - 1, 1)
    swap(last, STEPS[0])
    products(last - 1, 2)
    swap(last, STEPS[1])
    swap(last, STEPS[2])
    swapped(shares - 1)

    scale = None
    for r in range(rounds + 1):
        tops = []
        for i in range(2 * SIDE):
            if r < rounds:
                tops.append(jnp.max(multiply(last, r, i), axis=0))
            if r:
                code(r - 1, 2 * i, scale)
                code(r - 1, 2 * i + 1, scale)
        if r < rounds:
            scale = scale_of(r, jnp.stack(tops))
        if r:
            for d1 in STEPS:
                back.phase_one(r - 1, d1)
            back.phase_two(r - 1, 0)

    def scale_send_along(axis):
        at = tuple(ALL if other < axis else place[other] for other in range(3))
        here = scales.at[(ALL, *at)]
        copies = []
        for step in STEPS:
            copy = pltpu.make_async_remote_copy(
                src_ref=here,
                dst_ref=here,
                send_sem=scale_send.at[axis, step],
                recv_sem=scale_recv.at[axis, step],
                device_id=neighbour(place, core, axis, step),
                device_id_type=MESH,
            )
            copy.start()
            copies.append(copy)
        return copies

    kept = pltpu.make_async_copy(
        largest.at[:, pl.ds(0, 1)], scales.at[(ALL, *place)], scale_keep
    )
    kept.start()
    kept.wait()
    shared = scale_send_along(0)
    for d1 in STEPS:
        for t in range(3):
            back.arrive(back.one[t, d1], d1)
            back.phase_two(t, d1)
    for copy in shared[:3]:
        copy.wait_recv()
    shared += scale_send_along(1)
    for d2 in (0,) + STEPS:
        for t in range(3):
            back.phase_three(t, d2)
    for copy in shared[3:6]:
        copy.wait_recv()
    shared += scale_send_along(2)
    for d2 in (0,) + STEPS:
        for d3 in (0,) + STEPS:
            for t in range(3):
                back.arrive(back.three[t, d2, d3], d3)
    for copy in shared[6:]:
        copy.wait_recv()
    for copy in shared:
        copy.wait_send()
    for exchange in into:
        exchange.finish()
    back.finish()
    for _, copy in swaps:
        copy.wait_send()


def decode_kernel(codes, scales, o_ref, held, scale, value, held_sem, scale_sem, value_sem):
    rounds, _, parts, _, n = held.shape
    blocks = [(r, slice(None), pl.ds(q, 1)) for r in range(rounds) for q in range(parts)]
    factors = pltpu.make_async_copy(scales, scale, scale_sem)
    loads = [
        pltpu.make_async_copy(codes.at[at], held.at[at], held_sem.at[k])
        for k, at in enumerate(blocks)
    ]
    stores = [
        pltpu.make_async_copy(value.at[at], o_ref.at[(at[0], 0, *at[1:])], value_sem.at[k])
        for k, at in enumerate(blocks)
    ]
    factors.start()
    for copy in loads:
        copy.start()
    factors.wait()
    for k in range(len(blocks)):
        r, q = k // parts, k % parts
        loads[k].wait()
        share = jnp.swapaxes(held[r, :, q], 0, 1)
        share = share.astype(jnp.int32).astype(jnp.float32) * (1.0 / CODES)
        root = share * share * (share * jnp.abs(share))
        value[r, :, q] = root * scale[r].reshape(1, -1, n)
        stores[k].start()
    for copy in stores:
        copy.wait()


def decode(codes, scales):
    rounds, f, parts, rows, n = codes.shape
    sems = pltpu.SemaphoreType.DMA
    return pl.pallas_call(
        decode_kernel,
        out_shape=jax.ShapeDtypeStruct((rounds, 1, rows, parts, f, n), jnp.float32),
        in_specs=[pl.BlockSpec(memory_space=pl.ANY)] * 2,
        out_specs=pl.BlockSpec(memory_space=pl.ANY),
        scratch_shapes=[
            pltpu.VMEM(codes.shape, codes.dtype),
            pltpu.VMEM(scales.shape, scales.dtype),
            pltpu.VMEM((rounds, rows, parts, f, n), jnp.float32),
            sems((rounds * parts,)),
            sems,
            sems((rounds * parts,)),
        ],
        compiler_params=pltpu.CompilerParams(vmem_limit_bytes=60 << 20),
        name="decode",
    )(codes, scales)


def cross(x, partners):
    windows, _, _, n = x.shape
    rows = n // 8
    grid = (SIDE, SIDE)
    sems = pltpu.SemaphoreType.DMA
    exchange_sems = [sems((3, 4)), sems((3, 4))] + [sems((3, 4, 4))] * 4
    return pl.pallas_call(
        kernel,
        out_shape=[
            jax.ShapeDtypeStruct((3, SIDE, *grid, 2, rows, n), jnp.int16),
            jax.ShapeDtypeStruct((3, SIDE, *grid, 1, n), jnp.float32),
        ],
        in_specs=[
            pl.BlockSpec(memory_space=pltpu.SMEM),
            pl.BlockSpec(memory_space=pl.ANY),
        ],
        out_specs=[pl.BlockSpec(memory_space=pl.ANY)] * 2,
        scratch_shapes=[pltpu.VMEM((4, 16, 2, SIDE**3, n), jnp.bfloat16)]
        + [pltpu.VMEM((3, SIDE, *grid, 2, share, n), jnp.bfloat16) for share in SHARES] * 3
        + [pltpu.VMEM((2, 3, SIDE, *grid, 2, share, n), jnp.bfloat16) for share in SHARES]
        + [
            pltpu.VMEM((8, 2 * n, 24 * max(SHARES)), jnp.bfloat16),
            pltpu.VMEM((3, SIDE, *grid, 2, rows, n), jnp.float32),
            pltpu.VMEM((3, 8, n), jnp.float32),
        ]
        + [pltpu.VMEM((3, SIDE, *grid, 2, rows, n), jnp.int16)] * 3
        + [sems((4,)), sems, sems((3, 4)), sems((3, 4))]
        + [sems((3, 4, 4))] * (2 * len(SHARES))
        + exchange_sems * (len(SHARES) + 1),
        compiler_params=pltpu.CompilerParams(
            collective_id=0, has_side_effects=True, vmem_limit_bytes=60 << 20
        ),
        cost_estimate=pl.CostEstimate(
            flops=24 * 8 * windows * n * n * 8,
            bytes_accessed=16 << 20,
            transcendentals=0,
        ),
        name="cross",
    )(partners, x)


def shards(spectra, partners):
    w, _, f, n = spectra.shape
    codes, scales = cross(spectra, partners)
    return decode(codes.reshape(3, f, 2, n // 8, n), scales.reshape(3, f, 1, n))


def solution(mesh):
    return jax.shard_map(
        shards,
        mesh=mesh,
        in_specs=(P("win", None, None, "blk"), P()),
        out_specs=P(None, "blk", "win", None, None, None),
        check_vma=False,
    )
```

```python
import functools

import jax
import jax.numpy as jnp
from jax import lax
from jax.experimental import pallas as pl
from jax.experimental.pallas import tpu as pltpu
from jax.sharding import PartitionSpec as P

MESH = pl.DeviceIdType.MESH
SIDE = 4
STEPS = (1, 3, 2)
ALL = slice(None)
SHARES = (48, 32)
CODES = 32767.0
TINY = 1e-36


def position():
    blk, win = lax.axis_index("blk"), lax.axis_index("win")
    return (win % 4, win // 4 * 2 + blk // 2 % 2, blk // 4), blk % 2


def device(place, core):
    x, y, z = place
    return (z * 4 + y % 2 * 2 + core, y // 2 * 4 + x)


def neighbour(place, core, axis, step):
    moved = list(place)
    moved[axis] = (moved[axis] + step) % SIDE
    return device(moved, core)


def pick(**chosen):
    return tuple(chosen.get(name, ALL) for name in "xyz")


def encode(value, scale):
    share = jnp.abs(value) * scale + 1e-20
    root = share * lax.rsqrt(share)
    root = root * lax.rsqrt(root)
    code = (root * CODES + 0.5).astype(jnp.int32)
    return jnp.where(value < 0, -code, code).astype(jnp.int16)


class Exchange:
    def __init__(self, place, core, source, first, second, target, sems):
        self.place, self.core = place, core
        self.source, self.first, self.second, self.target = source, first, second, target
        self.sems = sems
        self.one, self.two, self.three, self.kept, self.sent = {}, {}, {}, {}, []

    def send(self, src, dst, which, at, axis, step):
        send_sem, recv_sem = self.sems[2 * which], self.sems[2 * which + 1]
        copy = pltpu.make_async_remote_copy(
            src_ref=src,
            dst_ref=dst,
            send_sem=send_sem.at[at],
            recv_sem=recv_sem.at[at],
            device_id=neighbour(self.place, self.core, axis, step),
            device_id_type=MESH,
        )
        copy.start()
        self.sent.append((which, copy))
        return copy

    def keep(self, src, dst, which, at):
        copy = pltpu.make_async_copy(src, dst, self.sems[2 * which + 1].at[at])
        copy.start()
        return copy

    def axes(self, t):
        return t, (t + 1) % 3, (t + 2) % 3

    def phase_one(self, t, d1):
        a1, _, _ = self.axes(t)
        there = (self.place[a1] + d1) % SIDE
        self.one[t, d1] = self.send(
            self.source(t, pick(**{"xyz"[a1]: there})),
            self.first.at[t, self.place[a1]],
            0,
            (t, d1),
            a1,
            d1,
        )

    def phase_two(self, t, d1):
        a1, a2, _ = self.axes(t)
        origin = (self.place[a1] - d1) % SIDE
        for d2 in STEPS + (0,):
            there = (self.place[a2] + d2) % SIDE
            if d1 == 0:
                src = self.source(t, pick(**{"xyz"[a1]: origin, "xyz"[a2]: there}))
            else:
                rest = [there if axis == a2 else ALL for axis in range(3) if axis != a1]
                src = self.first.at[(t, origin, *rest)]
            dst = self.second.at[t, self.place[a2], origin]
            at = (t, d1, d2)
            if d2 == 0:
                self.two[at] = self.keep(src, dst, 1, at)
            else:
                self.two[at] = self.send(src, dst, 1, at, a2, d2)

    def phase_three(self, t, d2):
        a1, a2, a3 = self.axes(t)
        origin = (self.place[a2] - d2) % SIDE
        for d1 in (0,) + STEPS:
            self.arrive(self.two[t, d1, d2], d2)
        for d3 in STEPS + (0,):
            there = (self.place[a3] + d3) % SIDE
            src = self.second.at[t, origin, :, there]
            dst = self.target(t, pick(**{"xyz"[a2]: origin, "xyz"[a3]: self.place[a3]}))
            at = (t, d2, d3)
            if d3 == 0:
                self.three[at] = self.keep(src, dst, 2, at)
            else:
                self.three[at] = self.send(src, dst, 2, at, a3, d3)

    def landed(self, t, d2, d3):
        _, a2, a3 = self.axes(t)
        return pick(
            **{
                "xyz"[a2]: (self.place[a2] - d2) % SIDE,
                "xyz"[a3]: (self.place[a3] - d3) % SIDE,
            }
        )

    def arrive(self, copy, step):
        if step == 0:
            copy.wait()
        else:
            copy.wait_recv()

    def finish(self, before=3):
        for which, copy in self.sent:
            if which < before:
                copy.wait_send()
        self.sent = [(which, copy) for which, copy in self.sent if which >= before]


def kernel(mates, spectra, o_ref, scales, *scratch):
    scratch = list(scratch)

    def take(count):
        taken = scratch[:count]
        del scratch[:count]
        return taken

    (stage,) = take(1)
    shares = len(SHARES)
    last = shares - 1
    ready, first, second, every = take(shares), take(shares), take(shares), take(shares)
    turned, product, largest, part, first_out, second_out = take(6)
    stage_sem, scale_keep, scale_send, scale_recv = take(4)
    swap_send, swap_recv = take(shares), take(shares)
    place, core = position()
    sibling = device(place, 1 - core)
    rounds, n = product.shape[0], product.shape[-1]
    slots, cut_rows = stage.shape[:2]
    third = sum(SHARES)
    order = [
        (h, t, t * third + sum(SHARES[:h]) + k * cut_rows, k * cut_rows)
        for h in range(shares)
        for t in range(3)
        for k in range(SHARES[h] // cut_rows)
    ]

    def load(j):
        return pltpu.make_async_copy(
            spectra.at[pl.ds(order[j][2], cut_rows)],
            stage.at[j % slots],
            stage_sem.at[j % slots],
        )

    for j in range(slots):
        load(j).start()

    barrier = pltpu.get_barrier_semaphore()
    for axis in range(3):
        for step in STEPS:
            pl.semaphore_signal(
                barrier,
                inc=1,
                device_id=neighbour(place, core, axis, step),
                device_id_type=MESH,
            )
    pl.semaphore_signal(barrier, inc=1, device_id=sibling, device_id_type=MESH)

    def relayout(share, thirds):
        for j, (h, t, _, row) in enumerate(order):
            if h != share or t not in thirds:
                continue
            load(j).wait()

            @pl.loop(0, 2)
            def turn(q):
                for x in range(SIDE):
                    v = stage[j % slots, :, q, x * 16 : (x + 1) * 16, :]
                    v = jnp.swapaxes(v, 0, 1).reshape(SIDE, SIDE, cut_rows, n)
                    ready[h][t, x, :, :, q, row : row + cut_rows, :] = v

            if j + slots < len(order):
                load(j + slots).start()

    into = [
        Exchange(
            place,
            core,
            lambda t, at, h=h: ready[h].at[(t, *at)],
            first[h],
            second[h],
            lambda t, at, h=h: every[h].at[(core, t, *at)],
            take(6),
        )
        for h in range(shares)
    ]
    back = Exchange(
        place,
        core,
        lambda t, at: part.at[(t, *at)],
        first_out,
        second_out,
        lambda t, at: o_ref.at[(t, *at)],
        take(6),
    )
    swaps = []

    def swap(h, d2):
        for d3 in (0,) + STEPS:
            for t in range(3):
                into[h].arrive(into[h].three[t, d2, d3], d3)
                here = every[h].at[(core, t, *into[h].landed(t, d2, d3))]
                copy = pltpu.make_async_remote_copy(
                    src_ref=here,
                    dst_ref=here,
                    send_sem=swap_send[h].at[t, d2, d3],
                    recv_sem=swap_recv[h].at[t, d2, d3],
                    device_id=sibling,
                    device_id_type=MESH,
                )
                copy.start()
                swaps.append((h, copy))

    def swapped(h):
        for share, copy in swaps:
            if share == h:
                copy.wait_recv()

    def wide(h, owner, y_lo, z):
        halves = []
        for q in range(2):
            rows = []
            for t in range(3):
                for y_hi in range(2):
                    for x in range(SIDE):
                        rows.append(every[h][owner, t, x, 2 * y_hi + y_lo, z, q])
            halves.append(jnp.concatenate(rows, axis=0))
        return jnp.concatenate(halves, axis=1)

    def turn(h, i):
        turned[i, :, : 24 * SHARES[h]] = wide(h, core, i % 2, i // 2).T

    def multiply(h, r, i):
        depth = 24 * SHARES[h]
        z, y_lo = i // 2, i % 2
        if r == 0 and h != last:
            turn(h, i)
        mate = mates[r, i * 2 + core]
        g = jnp.dot(
            turned[i, :, :depth],
            wide(h, mate % 2, mate // 2 % 2, mate // 4),
            preferred_element_type=jnp.float32,
        )
        sums = (g[:n, :n] + g[n:, n:], g[:n, n:] - g[n:, :n])
        rows = product.shape[-2]
        at = lambda k: (r, k % SIDE, k // SIDE * 2 + y_lo, z)
        if h:
            old = [
                jnp.concatenate([product[(*at(k), q)] for k in range(2 * SIDE)], axis=0)
                for q in range(2)
            ]
            sums = (sums[0] + old[0], sums[1] + old[1])
        for k in range(2 * SIDE):
            for q in range(2):
                product[(*at(k), q)] = sums[q][k * rows : (k + 1) * rows]
        return jnp.maximum(jnp.abs(sums[0]), jnp.abs(sums[1])).reshape(-1, 8, n)

    def products(h, r):
        @pl.loop(0, 2)
        def blocks(j):
            for k in range(SIDE):
                multiply(h, r, j * SIDE + k)

    def code(r, i, scale):
        for z in range(SIDE):
            for q in range(2):
                part[r, i // SIDE, i % SIDE, z, q] = encode(
                    product[r, i // SIDE, i % SIDE, z, q], scale
                )

    def scale_of(r, top):
        top = jnp.maximum(jnp.max(jnp.max(top, axis=0), keepdims=True), TINY)
        largest[r] = jnp.broadcast_to(top, largest.shape[1:])
        return 1.0 / jnp.broadcast_to(top, (1, n))

    for h in range(shares):
        for thirds in ((0,), (1,), (2,)) if h == 0 else ((0, 1, 2),):
            relayout(h, thirds)
            if h == 0 and thirds[0] == 0:
                pl.semaphore_wait(barrier, 10)
            for d1 in STEPS:
                for t in thirds:
                    into[h].phase_one(t, d1)
        for t in range(3):
            into[h].phase_two(t, 0)
    for h in range(shares):
        for d1 in STEPS:
            for t in range(3):
                into[h].arrive(into[h].one[t, d1], d1)
                into[h].phase_two(t, d1)
    for h in range(shares):
        if h >= 2:
            for d2 in (0,) + STEPS:
                swap(h - 2, d2)
            swapped(h - 2)
            for r in range(rounds):
                products(h - 2, r)
        for d2 in (0,) + STEPS:
            for t in range(3):
                into[h].phase_three(t, d2)
    for d2 in (0,) + STEPS:
        swap(last - 1, d2)
    swapped(last - 1)
    products(last - 1, 0)
    swap(last, 0)
    products(last - 1, 1)
    swap(last, STEPS[0])
    products(last - 1, 2)
    swap(last, STEPS[1])
    swap(last, STEPS[2])
    for i in range(2 * SIDE):
        turn(last, i)
    swapped(last)

    scale = None
    for r in range(rounds + 1):
        tops = []
        for i in range(2 * SIDE):
            if r < rounds:
                tops.append(jnp.max(multiply(last, r, i), axis=0))
            if r:
                code(r - 1, 2 * i, scale)
                code(r - 1, 2 * i + 1, scale)
        if r < rounds:
            scale = scale_of(r, jnp.stack(tops))
        if r:
            for d1 in STEPS:
                back.phase_one(r - 1, d1)
            back.phase_two(r - 1, 0)

    def scale_send_along(axis):
        at = tuple(ALL if other < axis else place[other] for other in range(3))
        here = scales.at[(ALL, *at)]
        copies = []
        for step in STEPS:
            copy = pltpu.make_async_remote_copy(
                src_ref=here,
                dst_ref=here,
                send_sem=scale_send.at[axis, step],
                recv_sem=scale_recv.at[axis, step],
                device_id=neighbour(place, core, axis, step),
                device_id_type=MESH,
            )
            copy.start()
            copies.append(copy)
        return copies

    kept = pltpu.make_async_copy(
        largest.at[:, pl.ds(0, 1)], scales.at[(ALL, *place)], scale_keep
    )
    kept.start()
    kept.wait()
    shared = scale_send_along(0)
    for exchange in into:
        exchange.finish()
    for _, copy in swaps:
        copy.wait_send()
    for d1 in STEPS:
        for t in range(3):
            back.arrive(back.one[t, d1], d1)
            back.phase_two(t, d1)
    for copy in shared[:3]:
        copy.wait_recv()
    shared += scale_send_along(1)
    for d2 in (0,) + STEPS:
        for t in range(3):
            back.phase_three(t, d2)
    for copy in shared[3:6]:
        copy.wait_recv()
    shared += scale_send_along(2)
    for copy in shared[:6]:
        copy.wait_send()
    back.finish(2)
    for d2 in (0,) + STEPS:
        for d3 in (0,) + STEPS:
            for t in range(3):
                back.arrive(back.three[t, d2, d3], d3)
    for copy in shared[6:]:
        copy.wait_recv()
    for copy in shared[6:]:
        copy.wait_send()
    back.finish()


def decode_kernel(codes, scales, o_ref, held, scale, value, held_sem, scale_sem, value_sem):
    rounds, _, parts, _, n = held.shape
    blocks = [(r, slice(None), pl.ds(q, 1)) for r in range(rounds) for q in range(parts)]
    factors = pltpu.make_async_copy(scales, scale, scale_sem)
    loads = [
        pltpu.make_async_copy(codes.at[at], held.at[at], held_sem.at[k])
        for k, at in enumerate(blocks)
    ]
    stores = [
        pltpu.make_async_copy(value.at[at], o_ref.at[(at[0], 0, *at[1:])], value_sem.at[k])
        for k, at in enumerate(blocks)
    ]
    factors.start()
    for copy in loads:
        copy.start()
    factors.wait()
    for k in range(len(blocks)):
        r, q = k // parts, k % parts
        loads[k].wait()
        share = jnp.swapaxes(held[r, :, q], 0, 1)
        share = share.astype(jnp.int32).astype(jnp.float32) * (1.0 / CODES)
        root = share * share * (share * jnp.abs(share))
        value[r, :, q] = root * scale[r].reshape(1, -1, n)
        stores[k].start()
    for copy in stores:
        copy.wait()


def decode(codes, scales):
    rounds, f, parts, rows, n = codes.shape
    sems = pltpu.SemaphoreType.DMA
    return pl.pallas_call(
        decode_kernel,
        out_shape=jax.ShapeDtypeStruct((rounds, 1, rows, parts, f, n), jnp.float32),
        in_specs=[pl.BlockSpec(memory_space=pl.ANY)] * 2,
        out_specs=pl.BlockSpec(memory_space=pl.ANY),
        scratch_shapes=[
            pltpu.VMEM(codes.shape, codes.dtype),
            pltpu.VMEM(scales.shape, scales.dtype),
            pltpu.VMEM((rounds, rows, parts, f, n), jnp.float32),
            sems((rounds * parts,)),
            sems,
            sems((rounds * parts,)),
        ],
        compiler_params=pltpu.CompilerParams(vmem_limit_bytes=60 << 20),
        name="decode",
    )(codes, scales)


def cross(x, partners):
    windows, _, _, n = x.shape
    rows = n // 8
    grid = (SIDE, SIDE)
    sems = pltpu.SemaphoreType.DMA
    exchange_sems = [sems((3, 4)), sems((3, 4))] + [sems((3, 4, 4))] * 4
    return pl.pallas_call(
        kernel,
        out_shape=[
            jax.ShapeDtypeStruct((3, SIDE, *grid, 2, rows, n), jnp.int16),
            jax.ShapeDtypeStruct((3, SIDE, *grid, 1, n), jnp.float32),
        ],
        in_specs=[
            pl.BlockSpec(memory_space=pltpu.SMEM),
            pl.BlockSpec(memory_space=pl.ANY),
        ],
        out_specs=[pl.BlockSpec(memory_space=pl.ANY)] * 2,
        scratch_shapes=[pltpu.VMEM((4, 16, 2, SIDE**3, n), jnp.bfloat16)]
        + [pltpu.VMEM((3, SIDE, *grid, 2, share, n), jnp.bfloat16) for share in SHARES] * 3
        + [pltpu.VMEM((2, 3, SIDE, *grid, 2, share, n), jnp.bfloat16) for share in SHARES]
        + [
            pltpu.VMEM((8, 2 * n, 24 * max(SHARES)), jnp.bfloat16),
            pltpu.VMEM((3, SIDE, *grid, 2, rows, n), jnp.float32),
            pltpu.VMEM((3, 8, n), jnp.float32),
        ]
        + [pltpu.VMEM((3, SIDE, *grid, 2, rows, n), jnp.int16)] * 3
        + [sems((4,)), sems, sems((3, 4)), sems((3, 4))]
        + [sems((3, 4, 4))] * (2 * len(SHARES))
        + exchange_sems * (len(SHARES) + 1),
        compiler_params=pltpu.CompilerParams(
            collective_id=0, has_side_effects=True, vmem_limit_bytes=60 << 20
        ),
        cost_estimate=pl.CostEstimate(
            flops=24 * 8 * windows * n * n * 8,
            bytes_accessed=16 << 20,
            transcendentals=0,
        ),
        name="cross",
    )(partners, x)


def shards(spectra, partners):
    w, _, f, n = spectra.shape
    codes, scales = cross(spectra, partners)
    return decode(codes.reshape(3, f, 2, n // 8, n), scales.reshape(3, f, 1, n))


def solution(mesh):
    return jax.shard_map(
        shards,
        mesh=mesh,
        in_specs=(P("win", None, None, "blk"), P()),
        out_specs=P(None, "blk", "win", None, None, None),
        check_vma=False,
    )
```

```python
import functools

import jax
import jax.numpy as jnp
from jax import lax
from jax.experimental import pallas as pl
from jax.experimental.pallas import tpu as pltpu
from jax.sharding import PartitionSpec as P

MESH = pl.DeviceIdType.MESH
SIDE = 4
STEPS = (1, 3, 2)
ALL = slice(None)
SHARES = (48, 32)
CODES = 32767.0
TINY = 1e-36


def position():
    blk, win = lax.axis_index("blk"), lax.axis_index("win")
    return (win % 4, win // 4 * 2 + blk // 2 % 2, blk // 4), blk % 2


def device(place, core):
    x, y, z = place
    return (z * 4 + y % 2 * 2 + core, y // 2 * 4 + x)


def neighbour(place, core, axis, step):
    moved = list(place)
    moved[axis] = (moved[axis] + step) % SIDE
    return device(moved, core)


def pick(**chosen):
    return tuple(chosen.get(name, ALL) for name in "xyz")


def encode(value, scale):
    share = jnp.abs(value) * scale + 1e-20
    root = share * lax.rsqrt(share)
    root = root * lax.rsqrt(root)
    code = (root * CODES + 0.5).astype(jnp.int32)
    return jnp.where(value < 0, -code, code).astype(jnp.int16)


class Exchange:
    def __init__(self, place, core, source, first, second, target, sems):
        self.place, self.core = place, core
        self.source, self.first, self.second, self.target = source, first, second, target
        self.sems = sems
        self.one, self.two, self.three, self.kept, self.sent = {}, {}, {}, {}, []

    def send(self, src, dst, which, at, axis, step):
        send_sem, recv_sem = self.sems[2 * which], self.sems[2 * which + 1]
        copy = pltpu.make_async_remote_copy(
            src_ref=src,
            dst_ref=dst,
            send_sem=send_sem.at[at],
            recv_sem=recv_sem.at[at],
            device_id=neighbour(self.place, self.core, axis, step),
            device_id_type=MESH,
        )
        copy.start()
        self.sent.append((which, copy))
        return copy

    def keep(self, src, dst, which, at):
        copy = pltpu.make_async_copy(src, dst, self.sems[2 * which + 1].at[at])
        copy.start()
        return copy

    def axes(self, t):
        return t, (t + 1) % 3, (t + 2) % 3

    def phase_one(self, t, d1):
        a1, _, _ = self.axes(t)
        there = (self.place[a1] + d1) % SIDE
        self.one[t, d1] = self.send(
            self.source(t, pick(**{"xyz"[a1]: there})),
            self.first.at[t, self.place[a1]],
            0,
            (t, d1),
            a1,
            d1,
        )

    def phase_two(self, t, d1):
        a1, a2, _ = self.axes(t)
        origin = (self.place[a1] - d1) % SIDE
        for d2 in STEPS + (0,):
            there = (self.place[a2] + d2) % SIDE
            if d1 == 0:
                src = self.source(t, pick(**{"xyz"[a1]: origin, "xyz"[a2]: there}))
            else:
                rest = [there if axis == a2 else ALL for axis in range(3) if axis != a1]
                src = self.first.at[(t, origin, *rest)]
            dst = self.second.at[t, self.place[a2], origin]
            at = (t, d1, d2)
            if d2 == 0:
                self.two[at] = self.keep(src, dst, 1, at)
            else:
                self.two[at] = self.send(src, dst, 1, at, a2, d2)

    def phase_three(self, t, d2):
        a1, a2, a3 = self.axes(t)
        origin = (self.place[a2] - d2) % SIDE
        for d1 in (0,) + STEPS:
            self.arrive(self.two[t, d1, d2], d2)
        for d3 in STEPS + (0,):
            there = (self.place[a3] + d3) % SIDE
            src = self.second.at[t, origin, :, there]
            dst = self.target(t, pick(**{"xyz"[a2]: origin, "xyz"[a3]: self.place[a3]}))
            at = (t, d2, d3)
            if d3 == 0:
                self.three[at] = self.keep(src, dst, 2, at)
            else:
                self.three[at] = self.send(src, dst, 2, at, a3, d3)

    def landed(self, t, d2, d3):
        _, a2, a3 = self.axes(t)
        return pick(
            **{
                "xyz"[a2]: (self.place[a2] - d2) % SIDE,
                "xyz"[a3]: (self.place[a3] - d3) % SIDE,
            }
        )

    def arrive(self, copy, step):
        if step == 0:
            copy.wait()
        else:
            copy.wait_recv()

    def finish(self, before=3):
        for which, copy in self.sent:
            if which < before:
                copy.wait_send()
        self.sent = [(which, copy) for which, copy in self.sent if which >= before]


def kernel(mates, spectra, o_ref, scales, *scratch):
    scratch = list(scratch)

    def take(count):
        taken = scratch[:count]
        del scratch[:count]
        return taken

    (stage,) = take(1)
    shares = len(SHARES)
    last = shares - 1
    ready, first, second, every = take(shares), take(shares), take(shares), take(shares)
    turned, product, largest, part, first_out, second_out = take(6)
    stage_sem, scale_keep, scale_send, scale_recv = take(4)
    swap_send, swap_recv = take(shares), take(shares)
    place, core = position()
    sibling = device(place, 1 - core)
    rounds, n = product.shape[0], product.shape[-1]
    slots, cut_rows = stage.shape[:2]
    third = sum(SHARES)
    order = [
        (h, t, t * third + sum(SHARES[:h]) + k * cut_rows, k * cut_rows)
        for h in range(shares)
        for t in range(3)
        for k in range(SHARES[h] // cut_rows)
    ]

    def load(j):
        return pltpu.make_async_copy(
            spectra.at[pl.ds(order[j][2], cut_rows)],
            stage.at[j % slots],
            stage_sem.at[j % slots],
        )

    for j in range(slots):
        load(j).start()

    barrier = pltpu.get_barrier_semaphore()
    for axis in range(3):
        for step in STEPS:
            pl.semaphore_signal(
                barrier,
                inc=1,
                device_id=neighbour(place, core, axis, step),
                device_id_type=MESH,
            )
    pl.semaphore_signal(barrier, inc=1, device_id=sibling, device_id_type=MESH)

    def relayout(share, thirds):
        for j, (h, t, _, row) in enumerate(order):
            if h != share or t not in thirds:
                continue
            load(j).wait()

            @pl.loop(0, 2)
            def turn(q):
                for x in range(SIDE):
                    v = stage[j % slots, :, q, x * 16 : (x + 1) * 16, :]
                    v = jnp.swapaxes(v, 0, 1).reshape(SIDE, SIDE, cut_rows, n)
                    ready[h][t, x, :, :, q, row : row + cut_rows, :] = v

            if j + slots < len(order):
                load(j + slots).start()

    into = [
        Exchange(
            place,
            core,
            lambda t, at, h=h: ready[h].at[(t, *at)],
            first[h],
            second[h],
            lambda t, at, h=h: every[h].at[(core, t, *at)],
            take(6),
        )
        for h in range(shares)
    ]
    back = Exchange(
        place,
        core,
        lambda t, at: part.at[(t, *at)],
        first_out,
        second_out,
        lambda t, at: o_ref.at[(t, *at)],
        take(6),
    )
    swaps = []

    def swap(h, d2):
        for d3 in (0,) + STEPS:
            for t in range(3):
                into[h].arrive(into[h].three[t, d2, d3], d3)
                here = every[h].at[(core, t, *into[h].landed(t, d2, d3))]
                copy = pltpu.make_async_remote_copy(
                    src_ref=here,
                    dst_ref=here,
                    send_sem=swap_send[h].at[t, d2, d3],
                    recv_sem=swap_recv[h].at[t, d2, d3],
                    device_id=sibling,
                    device_id_type=MESH,
                )
                copy.start()
                swaps.append((h, copy))

    def swapped(h):
        for share, copy in swaps:
            if share == h:
                copy.wait_recv()

    def wide(h, owner, y_lo, z):
        halves = []
        for q in range(2):
            rows = []
            for t in range(3):
                for y_hi in range(2):
                    for x in range(SIDE):
                        rows.append(every[h][owner, t, x, 2 * y_hi + y_lo, z, q])
            halves.append(jnp.concatenate(rows, axis=0))
        return jnp.concatenate(halves, axis=1)

    def turn(h, i):
        turned[i, :, : 24 * SHARES[h]] = wide(h, core, i % 2, i // 2).T

    def turn_all(h):
        @pl.loop(0, 2)
        def blocks(j):
            for k in range(SIDE):
                turn(h, j * SIDE + k)

    def multiply(h, r, i):
        depth = 24 * SHARES[h]
        z, y_lo = i // 2, i % 2
        mate = mates[r, i * 2 + core]
        g = jnp.dot(
            turned[i, :, :depth],
            wide(h, mate % 2, mate // 2 % 2, mate // 4),
            preferred_element_type=jnp.float32,
        )
        sums = (g[:n, :n] + g[n:, n:], g[:n, n:] - g[n:, :n])
        rows = product.shape[-2]
        at = lambda k: (r, k % SIDE, k // SIDE * 2 + y_lo, z)
        if h:
            old = [
                jnp.concatenate([product[(*at(k), q)] for k in range(2 * SIDE)], axis=0)
                for q in range(2)
            ]
            sums = (sums[0] + old[0], sums[1] + old[1])
        for k in range(2 * SIDE):
            for q in range(2):
                product[(*at(k), q)] = sums[q][k * rows : (k + 1) * rows]
        return jnp.maximum(jnp.abs(sums[0]), jnp.abs(sums[1])).reshape(-1, 8, n)

    def products(h, r):
        @pl.loop(0, 2)
        def blocks(j):
            for k in range(SIDE):
                multiply(h, r, j * SIDE + k)

    def code(r, i, scale):
        for z in range(SIDE):
            for q in range(2):
                part[r, i // SIDE, i % SIDE, z, q] = encode(
                    product[r, i // SIDE, i % SIDE, z, q], scale
                )

    def scale_of(r, top):
        top = jnp.maximum(jnp.max(jnp.max(top, axis=0), keepdims=True), TINY)
        largest[r] = jnp.broadcast_to(top, largest.shape[1:])
        return 1.0 / jnp.broadcast_to(top, (1, n))

    for h in range(shares):
        for thirds in ((0,), (1,), (2,)) if h == 0 else ((0, 1, 2),):
            relayout(h, thirds)
            if h == 0 and thirds[0] == 0:
                pl.semaphore_wait(barrier, 10)
            for d1 in STEPS:
                for t in thirds:
                    into[h].phase_one(t, d1)
        for t in range(3):
            into[h].phase_two(t, 0)
    for h in range(shares):
        for d1 in STEPS:
            for t in range(3):
                into[h].arrive(into[h].one[t, d1], d1)
                into[h].phase_two(t, d1)
    for h in range(shares):
        if h >= 2:
            for d2 in (0,) + STEPS:
                swap(h - 2, d2)
            turn_all(h - 2)
            swapped(h - 2)
            for r in range(rounds):
                products(h - 2, r)
        for d2 in (0,) + STEPS:
            for t in range(3):
                into[h].phase_three(t, d2)
    for d2 in (0,) + STEPS:
        swap(last - 1, d2)
    turn_all(last - 1)
    swapped(last - 1)
    products(last - 1, 0)
    swap(last, 0)
    products(last - 1, 1)
    swap(last, STEPS[0])
    products(last - 1, 2)
    swap(last, STEPS[1])
    swap(last, STEPS[2])
    for i in range(2 * SIDE):
        turn(last, i)
    swapped(last)

    scale = None
    for r in range(rounds + 1):
        tops = []
        for i in range(2 * SIDE):
            if r < rounds:
                tops.append(jnp.max(multiply(last, r, i), axis=0))
            if r:
                code(r - 1, 2 * i, scale)
                code(r - 1, 2 * i + 1, scale)
        if r < rounds:
            scale = scale_of(r, jnp.stack(tops))
        if r:
            for d1 in STEPS:
                back.phase_one(r - 1, d1)
            back.phase_two(r - 1, 0)

    def scale_send_along(axis):
        at = tuple(ALL if other < axis else place[other] for other in range(3))
        here = scales.at[(ALL, *at)]
        copies = []
        for step in STEPS:
            copy = pltpu.make_async_remote_copy(
                src_ref=here,
                dst_ref=here,
                send_sem=scale_send.at[axis, step],
                recv_sem=scale_recv.at[axis, step],
                device_id=neighbour(place, core, axis, step),
                device_id_type=MESH,
            )
            copy.start()
            copies.append(copy)
        return copies

    kept = pltpu.make_async_copy(
        largest.at[:, pl.ds(0, 1)], scales.at[(ALL, *place)], scale_keep
    )
    kept.start()
    kept.wait()
    shared = scale_send_along(0)
    for exchange in into:
        exchange.finish()
    for _, copy in swaps:
        copy.wait_send()
    for d1 in STEPS:
        for t in range(3):
            back.arrive(back.one[t, d1], d1)
            back.phase_two(t, d1)
    for copy in shared[:3]:
        copy.wait_recv()
    shared += scale_send_along(1)
    for d2 in (0,) + STEPS:
        for t in range(3):
            back.phase_three(t, d2)
    for copy in shared[3:6]:
        copy.wait_recv()
    shared += scale_send_along(2)
    for copy in shared[:6]:
        copy.wait_send()
    back.finish(2)
    for d2 in (0,) + STEPS:
        for d3 in (0,) + STEPS:
            for t in range(3):
                back.arrive(back.three[t, d2, d3], d3)
    for copy in shared[6:]:
        copy.wait_recv()
    for copy in shared[6:]:
        copy.wait_send()
    back.finish()


def decode_kernel(codes, scales, o_ref, held, scale, value, held_sem, scale_sem, value_sem):
    rounds, _, parts, _, n = held.shape
    blocks = [(r, slice(None), pl.ds(q, 1)) for r in range(rounds) for q in range(parts)]
    factors = pltpu.make_async_copy(scales, scale, scale_sem)
    loads = [
        pltpu.make_async_copy(codes.at[at], held.at[at], held_sem.at[k])
        for k, at in enumerate(blocks)
    ]
    stores = [
        pltpu.make_async_copy(value.at[at], o_ref.at[(at[0], 0, *at[1:])], value_sem.at[k])
        for k, at in enumerate(blocks)
    ]
    factors.start()
    for copy in loads:
        copy.start()
    factors.wait()
    for k in range(len(blocks)):
        r, q = k // parts, k % parts
        loads[k].wait()
        share = jnp.swapaxes(held[r, :, q], 0, 1)
        share = share.astype(jnp.int32).astype(jnp.float32) * (1.0 / CODES)
        root = share * share * (share * jnp.abs(share))
        value[r, :, q] = root * scale[r].reshape(1, -1, n)
        stores[k].start()
    for copy in stores:
        copy.wait()


def decode(codes, scales):
    rounds, f, parts, rows, n = codes.shape
    sems = pltpu.SemaphoreType.DMA
    return pl.pallas_call(
        decode_kernel,
        out_shape=jax.ShapeDtypeStruct((rounds, 1, rows, parts, f, n), jnp.float32),
        in_specs=[pl.BlockSpec(memory_space=pl.ANY)] * 2,
        out_specs=pl.BlockSpec(memory_space=pl.ANY),
        scratch_shapes=[
            pltpu.VMEM(codes.shape, codes.dtype),
            pltpu.VMEM(scales.shape, scales.dtype),
            pltpu.VMEM((rounds, rows, parts, f, n), jnp.float32),
            sems((rounds * parts,)),
            sems,
            sems((rounds * parts,)),
        ],
        compiler_params=pltpu.CompilerParams(vmem_limit_bytes=60 << 20),
        name="decode",
    )(codes, scales)


def cross(x, partners):
    windows, _, _, n = x.shape
    rows = n // 8
    grid = (SIDE, SIDE)
    sems = pltpu.SemaphoreType.DMA
    exchange_sems = [sems((3, 4)), sems((3, 4))] + [sems((3, 4, 4))] * 4
    return pl.pallas_call(
        kernel,
        out_shape=[
            jax.ShapeDtypeStruct((3, SIDE, *grid, 2, rows, n), jnp.int16),
            jax.ShapeDtypeStruct((3, SIDE, *grid, 1, n), jnp.float32),
        ],
        in_specs=[
            pl.BlockSpec(memory_space=pltpu.SMEM),
            pl.BlockSpec(memory_space=pl.ANY),
        ],
        out_specs=[pl.BlockSpec(memory_space=pl.ANY)] * 2,
        scratch_shapes=[pltpu.VMEM((4, 16, 2, SIDE**3, n), jnp.bfloat16)]
        + [pltpu.VMEM((3, SIDE, *grid, 2, share, n), jnp.bfloat16) for share in SHARES] * 3
        + [pltpu.VMEM((2, 3, SIDE, *grid, 2, share, n), jnp.bfloat16) for share in SHARES]
        + [
            pltpu.VMEM((8, 2 * n, 24 * max(SHARES)), jnp.bfloat16),
            pltpu.VMEM((3, SIDE, *grid, 2, rows, n), jnp.float32),
            pltpu.VMEM((3, 8, n), jnp.float32),
        ]
        + [pltpu.VMEM((3, SIDE, *grid, 2, rows, n), jnp.int16)] * 3
        + [sems((4,)), sems, sems((3, 4)), sems((3, 4))]
        + [sems((3, 4, 4))] * (2 * len(SHARES))
        + exchange_sems * (len(SHARES) + 1),
        compiler_params=pltpu.CompilerParams(
            collective_id=0, has_side_effects=True, vmem_limit_bytes=60 << 20
        ),
        cost_estimate=pl.CostEstimate(
            flops=24 * 8 * windows * n * n * 8,
            bytes_accessed=16 << 20,
            transcendentals=0,
        ),
        name="cross",
    )(partners, x)


def shards(spectra, partners):
    w, _, f, n = spectra.shape
    codes, scales = cross(spectra, partners)
    return decode(codes.reshape(3, f, 2, n // 8, n), scales.reshape(3, f, 1, n))


def solution(mesh):
    return jax.shard_map(
        shards,
        mesh=mesh,
        in_specs=(P("win", None, None, "blk"), P()),
        out_specs=P(None, "blk", "win", None, None, None),
        check_vma=False,
    )
```
